128 devices in a mesh: row: 16 (over z, y_hi, core), col: 8 (over x, y_lo).
Axes of the slice: x: 4, y: 4 (y_hi: 2, y_lo: 2; y = y_hi * 2 + y_lo), z: 4, core: 2. Of those that a mesh axis runs over, the one named last changes fastest.
Arguments:
- hamiltonian: bfloat16 [6144, 6144], P('row', 'col'), may hold values from -6 to 6, as said below
- density: bfloat16 [6144, 6144], P('row', 'col'), as said below
- h_pattern: int32 [96, 96], P('row', 'col'), may hold values from 0 to 1, as said below
- p_pattern: int32 [96, 96], P('row', 'col'), may hold values from 0 to 1, as said below
- keep_mask: int32 [96, 96], P('row', 'col'), may hold values from 0 to 1, as said below
Outputs:
- gradient: float32 [6144, 6144], P('row', 'col')
The draws below stay inside these ranges and needn't reach their ends.
Inputs may be any that keep to these rules, and one draw needn't show every extreme that they name: `hamiltonian`: Symmetric. `density`: Symmetric. `h_pattern`: each entry is 0 or 1; symmetric; every diagonal entry is 1, and the share of ones falls with the distance between block indices. `p_pattern`: each entry is 0 or 1; symmetric; every diagonal entry is 1, and the share of ones falls with the distance between block indices. `keep_mask`: each entry is 0 or 1; symmetric; every diagonal entry is 1, and the share of ones falls with the distance between block indices.
All inputs are finite; a program needn't handle non-finite values.
Results may differ from the reference program's by a relative error of at most 0.0003.
Values may be sent and summed in bfloat16 or wider, within the bound.
A program may use at most 128 MiB of HBM per device.

```python
import jax
import jax.numpy as jnp

NB = 96
NO = 6144


def banded(key):
    indices = jnp.arange(NB, dtype=jnp.int32)
    distance = jnp.abs(indices[:, None] - indices[None, :])
    ticket = jax.random.randint(key, (NB, NB), 0, NB, dtype=jnp.int32)
    upper = indices[:, None] <= indices[None, :]
    ticket = jnp.where(upper, ticket, ticket.T)
    return (ticket >= distance).astype(jnp.int32)


def mirrored(key, spread, limit):
    values = jax.random.normal(key, (NO, NO), jnp.float32)
    values = (values + values.T) * 0.70710678
    return jnp.clip(values, -limit, limit) * spread


def draw_hamiltonian(key, part):
    key = jax.random.fold_in(key, 5)
    return mirrored(key, 1.0, 6.0).astype(jnp.bfloat16)


def draw_density(key, part):
    key = jax.random.fold_in(key, 7)
    return mirrored(key, NO ** (-0.5), 6.0).astype(jnp.bfloat16)


def draw_h_pattern(key, part):
    key = jax.random.fold_in(key, 11)
    return banded(key)


def draw_p_pattern(key, part):
    key = jax.random.fold_in(key, 23)
    return banded(key)


def draw_keep_mask(key, part):
    key = jax.random.fold_in(key, 37)
    return banded(key)


def setup_inputs(seed: int = 0) -> dict:
    arg_keys = jax.random.split(jax.random.key(seed), 6)
    hamiltonian = draw_hamiltonian(jax.random.fold_in(arg_keys[5], 71), 0)
    density = draw_density(jax.random.fold_in(arg_keys[5], 71), 0)
    h_pattern = draw_h_pattern(jax.random.fold_in(arg_keys[5], 71), 0)
    p_pattern = draw_p_pattern(jax.random.fold_in(arg_keys[5], 71), 0)
    keep_mask = draw_keep_mask(jax.random.fold_in(arg_keys[5], 71), 0)
    return {"hamiltonian": hamiltonian, "density": density, "h_pattern": h_pattern, "p_pattern": p_pattern, "keep_mask": keep_mask}


def apply_blocks(matrix, pattern):
    block_count = pattern.shape[0]
    block_width = matrix.shape[0] // block_count
    blocks = matrix.reshape(block_count, block_width, block_count, block_width)
    blocks = blocks * pattern.astype(matrix.dtype)[:, None, :, None]
    return blocks.reshape(matrix.shape)


def reference(hamiltonian, density, h_pattern, p_pattern, keep_mask):
    masked_ham = apply_blocks(hamiltonian, h_pattern)
    masked_den = apply_blocks(density, p_pattern)
    forward = jnp.dot(masked_ham, masked_den, preferred_element_type=jnp.float32)
    backward = jnp.dot(masked_den, masked_ham, preferred_element_type=jnp.float32)
    return apply_blocks(forward - backward, keep_mask)
```

```python
import functools

import jax
import jax.numpy as jnp
from jax import lax
from jax.experimental import pallas as pl
from jax.experimental.pallas import tpu as pltpu
from jax.sharding import PartitionSpec as P

MESH = pl.DeviceIdType.MESH
ROWS = 384
COLS = 768
BLOCK = 64
HALF = 192
LOW = 112
HIGH = 272
WIDE = 256


def device_of(x, y, z, core):
    return (4 * z + 2 * (y // 2) + core, 2 * x + y % 2)


def spread(pattern):
    count = pattern.shape[1]
    block_of = lax.broadcasted_iota(jnp.int32, (count, COLS), 1) // BLOCK
    index = lax.broadcasted_iota(jnp.int32, (count, COLS), 0)
    select = jnp.where(block_of == index, 1.0, 0.0).astype(jnp.float32)
    return jnp.dot(pattern.astype(jnp.float32), select, preferred_element_type=jnp.float32)


def kernel(ham, den, h_pat, p_pat, keep, out, row, col, acc, send, recv):
    row_index = lax.axis_index("row")
    col_index = lax.axis_index("col")
    x, y_lo = col_index // 2, col_index % 2
    z, y_hi, core = row_index // 4, (row_index // 2) % 2, row_index % 2
    y = 2 * y_hi + y_lo
    right = device_of((x + 1) % 4, y, z, core)
    left = device_of((x + 3) % 4, y, z, core)
    up = device_of(x, y, (z + 1) % 4, core)
    down = device_of(x, y, (z + 3) % 4, core)
    beside = device_of(x, 2 * y_hi + 1 - y_lo, z, core)
    across = device_of(x, 2 * (1 - y_hi) + y_lo, z, core)
    sibling = device_of(x, y, z, 1 - core)

    barrier = pltpu.get_barrier_semaphore()
    partners = (right, left, up, down, beside, across, sibling)
    for partner in partners:
        pl.semaphore_signal(barrier, inc=1, device_id=partner, device_id_type=MESH)

    row_own = 2 * x + y_lo
    col_own = 2 * z + y_hi
    base = core * ROWS
    for matrix, (tile, pattern) in enumerate(((ham, h_pat), (den, p_pat))):
        mask = spread(pattern[...]).astype(jnp.bfloat16)
        for i in range(ROWS // BLOCK):
            rows = pl.ds(i * BLOCK, BLOCK)
            masked = tile[rows, :] * mask[i : i + 1, :]
            row[row_own, matrix, rows, :] = masked
            col[col_own, matrix, pl.ds(pl.multiple_of(base + i * BLOCK, BLOCK), BLOCK), :] = masked
    acc[...] = jnp.zeros_like(acc)
    pl.semaphore_wait(barrier, len(partners))

    started = []

    def copy(ref, target):
        index = len(started)
        made = pltpu.make_async_remote_copy(
            src_ref=ref,
            dst_ref=ref,
            send_sem=send.at[index],
            recv_sem=recv.at[index],
            device_id=target,
            device_id_type=MESH,
        )
        started.append(made)
        made.start()
        return made

    def row_part(k, first, last):
        return row.at[k, :, pl.ds(first, last - first), :]

    def col_part(k, first, last):
        start = pl.multiple_of(base + first, 16)
        return col.at[k, :, pl.ds(start, last - first), :]

    class Gather:
        def __init__(self, part, place, low, ahead, behind, partner):
            self.part, self.low = part, low
            self.place = place
            self.ahead, self.behind, self.partner = ahead, behind, partner

        def k(self, offset, other):
            low = 1 - self.low if other else self.low
            return 2 * ((self.place + offset) % 4) + low

        def send_both(self, other):
            k, part = self.k(0, other), self.part
            first = copy(part(k, 0, HALF), self.ahead)
            second = copy(part(k, HALF, ROWS), self.behind)
            third = copy(part(k, HALF, ROWS), self.ahead)
            fourth = copy(part(k, 0, HALF), self.behind)
            return first, second, third, fourth

        def send_partner(self):
            self.crossed = copy(self.part(self.k(0, False), 0, ROWS), self.partner)

        def forward(self, other, low, high):
            ahead = copy(self.part(self.k(3, other), 0, low), self.ahead)
            behind = copy(self.part(self.k(1, other), high, ROWS), self.behind)
            return ahead, behind

        def send_partner_far(self):
            self.crossed_far = copy(self.part(self.k(2, False), LOW, HIGH), self.partner)

    rows = Gather(row_part, x, y_lo, right, left, beside)
    cols = Gather(col_part, z, y_hi, up, down, across)

    def share(k):
        return copy(col_part(k, 0, ROWS), sibling)

    shared = []
    near = [g.send_both(False) for g in (rows, cols)]
    for g in (rows, cols):
        g.send_partner()
    shared.append(share(col_own))

    far = []
    for g, (first, second, third, fourth) in zip((rows, cols), near):
        first.wait_recv()
        second.wait_recv()
        far.append(g.forward(False, HALF, HALF))
    near_other = []
    for g in (rows, cols):
        g.crossed.wait_recv()
        near_other.append(g.send_both(True))
    shared.append(share(cols.k(0, True)))
    for g, (first, second, third, fourth) in zip((rows, cols), near):
        third.wait_recv()
        fourth.wait_recv()
    shared.append(share(cols.k(1, False)))
    shared.append(share(cols.k(3, False)))

    def phase_of(place, low, k):
        distance = (k // 2 - place + 4) % 4
        other = (k % 2 + low) % 2
        near_phase = jnp.where(distance == 0, 0, 2 * other)
        far_phase = 1 + 2 * other
        return jnp.where(distance == 2, far_phase, near_phase)

    def multiply(phase):
        @pl.loop(0, 8)
        def _(k):
            ready = jnp.maximum(phase_of(x, y_lo, k), phase_of(z, y_hi, k))

            @pl.when(ready == phase)
            def _():
                @pl.loop(0, COLS // WIDE)
                def _(j):
                    columns = pl.ds(pl.multiple_of(j * WIDE, WIDE), WIDE)
                    forward = jnp.dot(
                        row[k, 0], col[k, 1, :, columns], preferred_element_type=jnp.float32
                    )
                    backward = jnp.dot(
                        row[k, 1], col[k, 0, :, columns], preferred_element_type=jnp.float32
                    )
                    acc[:, columns] += forward - backward

    for made in shared:
        made.wait_recv()
    multiply(0)

    for g, (ahead, behind) in zip((rows, cols), far):
        ahead.wait_recv()
        behind.wait_recv()
        g.send_partner_far()
    last = share(cols.k(2, False))
    far_other = []
    for g, (first, second, third, fourth) in zip((rows, cols), near_other):
        first.wait_recv()
        second.wait_recv()
        far_other.append(g.forward(True, LOW, HIGH))
    last.wait_recv()
    multiply(1)

    for g, (first, second, third, fourth) in zip((rows, cols), near_other):
        third.wait_recv()
        fourth.wait_recv()
    shared = [share(cols.k(1, True)), share(cols.k(3, True))]
    for made in shared:
        made.wait_recv()
    multiply(2)

    for g, (ahead, behind) in zip((cols, rows), far_other[::-1]):
        ahead.wait_recv()
        behind.wait_recv()
        g.crossed_far.wait_recv()
        if g is cols:
            last = share(cols.k(2, True))
    last.wait_recv()
    multiply(3)

    mask = spread(keep[...])
    for i in range(ROWS // BLOCK):
        block_rows = pl.ds(i * BLOCK, BLOCK)
        out[block_rows, :] = acc[block_rows, :] * mask[i : i + 1, :]
    for made in started:
        made.wait_send()


COPIES = 36


def shards(hamiltonian, density, h_pattern, p_pattern, keep_mask):
    vmem = pl.BlockSpec(memory_space=pltpu.VMEM)
    return pl.pallas_call(
        kernel,
        out_shape=jax.ShapeDtypeStruct((ROWS, COLS), jnp.float32),
        in_specs=[vmem] * 5,
        out_specs=vmem,
        scratch_shapes=[
            pltpu.VMEM((8, 2, ROWS, COLS), jnp.bfloat16),
            pltpu.VMEM((8, 2, 2 * ROWS, COLS), jnp.bfloat16),
            pltpu.VMEM((ROWS, COLS), jnp.float32),
            pltpu.SemaphoreType.DMA((COPIES,)),
            pltpu.SemaphoreType.DMA((COPIES,)),
        ],
        compiler_params=pltpu.CompilerParams(
            collective_id=0, has_side_effects=True, vmem_limit_bytes=50 * 1024 * 1024
        ),
        name="commutator",
    )(hamiltonian, density, h_pattern, p_pattern, keep_mask)


def solution(mesh):
    return jax.shard_map(
        shards,
        mesh=mesh,
        in_specs=(
            P("row", "col"),
            P("row", "col"),
            P("row", "col"),
            P("row", "col"),
            P("row", "col"),
        ),
        out_specs=P("row", "col"),
        check_vma=False,
    )
```

```python
import jax
import jax.numpy as jnp
from jax import lax
from jax.experimental import pallas as pl
from jax.experimental.pallas import tpu as pltpu
from jax.sharding import PartitionSpec as P

MESH = pl.DeviceIdType.MESH
ROWS = 384
COLS = 768
BLOCK = 64
BLOCK_ROWS = ROWS // BLOCK
BLOCK_COLS = COLS // BLOCK
WIDE = 256
CUTS = (0, 112, 192, 272, 384)
CHUNKS = tuple(zip(CUTS[:-1], CUTS[1:]))
WHOLE = (0, ROWS)
MIDDLE = (112, 272)
COPIES = 96


def device_of(x, y, z, core):
    return (4 * z + 2 * (y // 2) + core, 2 * x + y % 2)


def spread(pattern):
    block_of = lax.broadcasted_iota(jnp.int32, (BLOCK_COLS, COLS), 1) // BLOCK
    index = lax.broadcasted_iota(jnp.int32, (BLOCK_COLS, COLS), 0)
    select = jnp.where(block_of == index, 1.0, 0.0).astype(jnp.float32)
    return jnp.dot(pattern.astype(jnp.float32), select, preferred_element_type=jnp.float32)


class Gather:
    def __init__(self, copy, part, place, low, ahead, behind, partner):
        self.copy, self.part, self.place, self.low = copy, part, place, low
        self.ahead, self.behind, self.partner = ahead, behind, partner
        self.from_behind, self.from_ahead = {}, {}
        self.far_from_behind, self.far_from_ahead = {}, {}
        self.crossed, self.crossed_far = {}, None

    def k(self, offset, other):
        low = 1 - self.low if other else self.low
        return 2 * ((self.place + offset) % 4) + low

    def piece(self, offset, other, span):
        return self.part(self.k(offset, other), *span)

    def send_ahead(self, other, c):
        made = self.copy(self.piece(0, other, CHUNKS[c]), self.ahead)
        self.from_behind[other, c] = made

    def send_behind(self, other, c):
        made = self.copy(self.piece(0, other, CHUNKS[c]), self.behind)
        self.from_ahead[other, c] = made

    def cross(self, c):
        self.crossed[c] = self.copy(self.piece(0, False, CHUNKS[c]), self.partner)

    def pass_ahead(self, other, c):
        made = self.copy(self.piece(3, other, CHUNKS[c]), self.ahead)
        self.far_from_behind[other, c] = made

    def pass_behind(self, other, c):
        made = self.copy(self.piece(1, other, CHUNKS[c]), self.behind)
        self.far_from_ahead[other, c] = made

    def cross_far(self):
        self.crossed_far = self.copy(self.piece(2, False, MIDDLE), self.partner)


def kernel(ham, den, h_pat, p_pat, keep, out, row, col, acc, tiles, pats, send, recv, load):
    row_index = lax.axis_index("row")
    col_index = lax.axis_index("col")
    x, y_lo = col_index // 2, col_index % 2
    z, y_hi, core = row_index // 4, (row_index // 2) % 2, row_index % 2
    y = 2 * y_hi + y_lo
    right = device_of((x + 1) % 4, y, z, core)
    left = device_of((x + 3) % 4, y, z, core)
    up = device_of(x, y, (z + 1) % 4, core)
    down = device_of(x, y, (z + 3) % 4, core)
    beside = device_of(x, 2 * y_hi + 1 - y_lo, z, core)
    across = device_of(x, 2 * (1 - y_hi) + y_lo, z, core)
    sibling = device_of(x, y, z, 1 - core)

    barrier = pltpu.get_barrier_semaphore()
    partners = (right, left, up, down, beside, across, sibling)
    for partner in partners:
        pl.semaphore_signal(barrier, inc=1, device_id=partner, device_id_type=MESH)

    loads = []
    pairs = (
        (h_pat, pats.at[0]),
        (ham, tiles.at[0]),
        (p_pat, pats.at[1]),
        (den, tiles.at[1]),
        (keep, pats.at[2]),
    )
    for i, (source, target) in enumerate(pairs):
        made = pltpu.make_async_copy(source, target, load.at[i])
        made.start()
        loads.append(made)

    row_own = 2 * x + y_lo
    col_own = 2 * z + y_hi
    base = core * ROWS
    for matrix in range(2):
        loads[2 * matrix].wait()
        loads[2 * matrix + 1].wait()
        mask = spread(pats[matrix]).astype(jnp.bfloat16)
        for i in range(BLOCK_ROWS):
            rows = pl.ds(i * BLOCK, BLOCK)
            masked = tiles[matrix, rows, :] * mask[i : i + 1, :]
            row[row_own, matrix, rows, :] = masked
            col[col_own, matrix, pl.ds(pl.multiple_of(base + i * BLOCK, BLOCK), BLOCK), :] = masked
    loads[4].wait()
    pl.semaphore_wait(barrier, len(partners))

    started = []

    def copy(ref, target):
        index = len(started)
        made = pltpu.make_async_remote_copy(
            src_ref=ref,
            dst_ref=ref,
            send_sem=send.at[index],
            recv_sem=recv.at[index],
            device_id=target,
            device_id_type=MESH,
        )
        started.append(made)
        made.start()
        return made

    def row_part(k, first, last):
        return row.at[k, :, pl.ds(first, last - first), :]

    def col_part(k, first, last):
        start = pl.multiple_of(base + first, 16)
        return col.at[k, :, pl.ds(start, last - first), :]

    rows = Gather(copy, row_part, x, y_lo, right, left, beside)
    cols = Gather(copy, col_part, z, y_hi, up, down, across)
    both = (rows, cols)
    shared = []

    def share(offset, other, span):
        shared.append(copy(cols.piece(offset, other, span), sibling))

    def wait_shared():
        for made in shared:
            made.wait_recv()
        shared.clear()

    def phase_of(place, low, k):
        distance = (k // 2 - place + 4) % 4
        other = (k % 2 + low) % 2
        near = jnp.where(distance == 0, 2, 3)
        own_ring = jnp.where(distance == 2, 1, 0)
        other_ring = jnp.where(distance == 2, 4, near)
        return jnp.where(other == 0, own_ring, other_ring)

    def multiply(phase):
        @pl.loop(0, 8)
        def _(k):
            ready = jnp.maximum(phase_of(x, y_lo, k), phase_of(z, y_hi, k))

            @pl.when(ready == phase)
            def _():
                @pl.loop(0, COLS // WIDE)
                def _(j):
                    columns = pl.ds(pl.multiple_of(j * WIDE, WIDE), WIDE)
                    forward = jnp.dot(
                        row[k, 0], col[k, 1, :, columns], preferred_element_type=jnp.float32
                    )
                    backward = jnp.dot(
                        row[k, 1], col[k, 0, :, columns], preferred_element_type=jnp.float32
                    )
                    acc[:, columns] += forward - backward

    for first, second in ((0, 3), (1, 2), (2, 1), (3, 0)):
        for g in both:
            g.send_ahead(False, first)
            g.send_behind(False, second)
            if first == 0:
                g.cross(0)
                g.cross(3)
    for g in both:
        g.cross(1)
        g.cross(2)
    share(0, False, WHOLE)
    acc[...] = jnp.zeros_like(acc)

    for first, second in ((0, 3), (1, 2)):
        for g in both:
            g.from_behind[False, first].wait_recv()
            g.pass_ahead(False, first)
            g.from_ahead[False, second].wait_recv()
            g.pass_behind(False, second)
    for c in (0, 3):
        for g in both:
            g.crossed[c].wait_recv()
            if c == 0:
                g.send_ahead(True, 0)
            else:
                g.send_behind(True, 3)
                g.send_ahead(True, 3)
                g.send_behind(True, 0)

    for first, second in ((2, 1), (3, 0)):
        for g in both:
            g.from_behind[False, first].wait_recv()
            g.from_ahead[False, second].wait_recv()
    share(3, False, WHOLE)
    share(1, False, WHOLE)
    wait_shared()
    multiply(0)

    for g in both:
        g.crossed[1].wait_recv()
        g.send_ahead(True, 1)
        g.send_behind(True, 1)
    for first, second in ((0, 3), (1, 2)):
        for g in both:
            g.far_from_behind[False, first].wait_recv()
            g.far_from_ahead[False, second].wait_recv()
    for g in both:
        g.cross_far()
    share(2, False, WHOLE)
    for g in both:
        g.crossed[2].wait_recv()
        g.send_ahead(True, 2)
        g.send_behind(True, 2)
    share(0, True, WHOLE)
    for g in both:
        g.from_behind[True, 0].wait_recv()
        g.pass_ahead(True, 0)
        g.from_ahead[True, 3].wait_recv()
        g.pass_behind(True, 3)
    wait_shared()
    multiply(1)
    multiply(2)

    for first, second in ((3, 0), (1, 1)):
        for g in both:
            g.from_behind[True, first].wait_recv()
            g.from_ahead[True, second].wait_recv()
    share(3, True, (0, 192))
    share(3, True, (272, 384))
    share(1, True, (0, 192))
    share(1, True, (272, 384))
    for g in both:
        g.from_behind[True, 2].wait_recv()
        g.from_ahead[True, 2].wait_recv()
    share(3, True, (192, 272))
    share(1, True, (192, 272))
    wait_shared()
    multiply(3)

    cols.crossed_far.wait_recv()
    share(2, True, MIDDLE)
    cols.far_from_behind[True, 0].wait_recv()
    share(2, True, CHUNKS[0])
    cols.far_from_ahead[True, 3].wait_recv()
    share(2, True, CHUNKS[3])
    rows.crossed_far.wait_recv()
    rows.far_from_behind[True, 0].wait_recv()
    rows.far_from_ahead[True, 3].wait_recv()
    wait_shared()
    multiply(4)

    mask = spread(pats[2])
    for i in range(BLOCK_ROWS):
        block_rows = pl.ds(i * BLOCK, BLOCK)
        out[block_rows, :] = acc[block_rows, :] * mask[i : i + 1, :]
    for made in started:
        made.wait_send()


def shards(hamiltonian, density, h_pattern, p_pattern, keep_mask):
    return pl.pallas_call(
        kernel,
        out_shape=jax.ShapeDtypeStruct((ROWS, COLS), jnp.float32),
        in_specs=[pl.BlockSpec(memory_space=pl.ANY)] * 5,
        out_specs=pl.BlockSpec(memory_space=pltpu.VMEM),
        scratch_shapes=[
            pltpu.VMEM((8, 2, ROWS, COLS), jnp.bfloat16),
            pltpu.VMEM((8, 2, 2 * ROWS, COLS), jnp.bfloat16),
            pltpu.VMEM((ROWS, COLS), jnp.float32),
            pltpu.VMEM((2, ROWS, COLS), jnp.bfloat16),
            pltpu.VMEM((3, BLOCK_ROWS, BLOCK_COLS), jnp.int32),
            pltpu.SemaphoreType.DMA((COPIES,)),
            pltpu.SemaphoreType.DMA((COPIES,)),
            pltpu.SemaphoreType.DMA((5,)),
        ],
        compiler_params=pltpu.CompilerParams(
            collective_id=0, has_side_effects=True, vmem_limit_bytes=60 * 1024 * 1024
        ),
        name="commutator",
    )(hamiltonian, density, h_pattern, p_pattern, keep_mask)


def solution(mesh):
    return jax.shard_map(
        shards,
        mesh=mesh,
        in_specs=(
            P("row", "col"),
            P("row", "col"),
            P("row", "col"),
            P("row", "col"),
            P("row", "col"),
        ),
        out_specs=P("row", "col"),
        check_vma=False,
    )
```

```python
import jax
import jax.numpy as jnp
from jax import lax
from jax.experimental import pallas as pl
from jax.experimental.pallas import tpu as pltpu
from jax.sharding import PartitionSpec as P

MESH = pl.DeviceIdType.MESH
ROWS = 384
COLS = 768
BLOCK = 64
BLOCK_ROWS = ROWS // BLOCK
BLOCK_COLS = COLS // BLOCK
CUTS = (0, 128, 192, 256, 384)
CHUNKS = tuple(zip(CUTS[:-1], CUTS[1:]))
WHOLE = (0, ROWS)
LOW = (0, 48)
MIDDLE = (48, 192)
UPPER = (192, 336)
HIGH = (336, 384)
COPIES = 96


def device_of(x, y, z, core):
    return (4 * z + 2 * (y // 2) + core, 2 * x + y % 2)


def spread(pattern):
    block_of = lax.broadcasted_iota(jnp.int32, (BLOCK_COLS, COLS), 1) // BLOCK
    index = lax.broadcasted_iota(jnp.int32, (BLOCK_COLS, COLS), 0)
    select = jnp.where(block_of == index, 1.0, 0.0).astype(jnp.float32)
    return jnp.dot(pattern.astype(jnp.float32), select, preferred_element_type=jnp.float32)


class Gather:
    def __init__(self, copy, part, place, low, ahead, behind):
        self.copy, self.part, self.place, self.low = copy, part, place, low
        self.ahead, self.behind = ahead, behind
        self.from_behind, self.from_ahead = {}, {}
        self.far_from_behind, self.far_from_ahead = {}, {}

    def k(self, offset, other):
        low = 1 - self.low if other else self.low
        return 2 * ((self.place + offset) % 4) + low

    def piece(self, offset, other, span):
        return self.part(self.k(offset, other), *span)

    def send_ahead(self, other, c):
        piece = self.piece(0, other, CHUNKS[c])
        self.from_behind[other, c] = self.copy(piece, piece, self.ahead)

    def send_behind(self, other, c):
        piece = self.piece(0, other, CHUNKS[c])
        self.from_ahead[other, c] = self.copy(piece, piece, self.behind)

    def pass_ahead(self, other, c, span):
        piece = self.piece(3, other, span)
        self.far_from_behind[other, c] = self.copy(piece, piece, self.ahead)

    def pass_behind(self, other, c, span):
        piece = self.piece(1, other, span)
        self.far_from_ahead[other, c] = self.copy(piece, piece, self.behind)


def kernel(ham, den, h_pat, p_pat, keep, out, row, col, acc, tiles, pats, send, recv, load):
    row_index = lax.axis_index("row")
    col_index = lax.axis_index("col")
    x, y_lo = col_index // 2, col_index % 2
    z, y_hi, core = row_index // 4, (row_index // 2) % 2, row_index % 2
    y = 2 * y_hi + y_lo
    right = device_of((x + 1) % 4, y, z, core)
    left = device_of((x + 3) % 4, y, z, core)
    up = device_of(x, y, (z + 1) % 4, core)
    down = device_of(x, y, (z + 3) % 4, core)
    beside = device_of(x, 2 * y_hi + 1 - y_lo, z, core)
    across = device_of(x, 2 * (1 - y_hi) + y_lo, z, core)
    opposite = device_of(x, 3 - y, z, core)
    sibling = device_of(x, y, z, 1 - core)

    barrier = pltpu.get_barrier_semaphore()
    partners = (right, left, up, down, beside, across, opposite, sibling)
    for partner in partners:
        pl.semaphore_signal(barrier, inc=1, device_id=partner, device_id_type=MESH)

    loads = []
    pairs = (
        (h_pat, pats.at[0]),
        (ham, tiles.at[0]),
        (p_pat, pats.at[1]),
        (den, tiles.at[1]),
        (keep, pats.at[2]),
    )
    for i, (source, target) in enumerate(pairs):
        made = pltpu.make_async_copy(source, target, load.at[i])
        made.start()
        loads.append(made)

    row_own = 2 * x + y_lo
    col_own = 2 * z + y_hi
    base = core * ROWS
    for matrix in range(2):
        loads[2 * matrix].wait()
        loads[2 * matrix + 1].wait()
        mask = spread(pats[matrix]).astype(jnp.bfloat16)
        for i in range(BLOCK_ROWS):
            rows = pl.ds(i * BLOCK, BLOCK)
            masked = tiles[matrix, rows, :] * mask[i : i + 1, :]
            row[row_own, matrix, rows, :] = masked
            col[col_own, matrix, pl.ds(pl.multiple_of(base + i * BLOCK, BLOCK), BLOCK), :] = masked
    loads[4].wait()
    pl.semaphore_wait(barrier, len(partners))

    started = []

    def copy(source, landing, target):
        index = len(started)
        made = pltpu.make_async_remote_copy(
            src_ref=source,
            dst_ref=landing,
            send_sem=send.at[index],
            recv_sem=recv.at[index],
            device_id=target,
            device_id_type=MESH,
        )
        started.append(made)
        made.start()
        return made

    def row_part(k, first, last):
        return row.at[k, :, pl.ds(first, last - first), :]

    def col_part(k, first, last):
        start = pl.multiple_of(base + first, 16)
        return col.at[k, :, pl.ds(start, last - first), :]

    rows = Gather(copy, row_part, x, y_lo, right, left)
    cols = Gather(copy, col_part, z, y_hi, up, down)
    both = (rows, cols)
    shared = []

    def share(offset, other, span):
        piece = cols.piece(offset, other, span)
        shared.append(copy(piece, piece, sibling))

    def wait_shared():
        for made in shared:
            made.wait_recv()
        shared.clear()

    crossed, turned = {}, {}

    def cross(c):
        piece = rows.piece(0, False, CHUNKS[c])
        crossed[c] = copy(piece, piece, beside)

    def turn(c):
        crossed[c].wait_recv()
        landing = col_part(col_own, *CHUNKS[c])
        turned[c] = copy(rows.piece(0, True, CHUNKS[c]), landing, opposite)

    def phase_of(place, low, k):
        distance = (k // 2 - place + 4) % 4
        other = (k % 2 + low) % 2
        late = jnp.where(distance == 2, 2, 1)
        return jnp.where((other == 0) | (distance == 0), 0, late)

    def multiply(phase):
        @pl.loop(0, 8)
        def _(k):
            ready = jnp.maximum(phase_of(x, y_lo, k), phase_of(z, y_hi, k))

            @pl.when(ready == phase)
            def _():
                forward = jnp.dot(row[k, 0], col[k, 1], preferred_element_type=jnp.float32)
                backward = jnp.dot(row[k, 1], col[k, 0], preferred_element_type=jnp.float32)
                acc[...] += forward - backward

    for first, second in ((0, 3), (1, 2)):
        for g in both:
            g.send_ahead(False, first)
            g.send_behind(False, second)
        cross(first)
        cross(second)
    share(0, False, WHOLE)
    acc[...] = jnp.zeros_like(acc)

    for first, second in ((0, 3), (1, 2)):
        for g in both:
            g.from_behind[False, first].wait_recv()
            g.pass_ahead(False, first, CHUNKS[first])
            g.from_ahead[False, second].wait_recv()
            g.pass_behind(False, second, CHUNKS[second])
        turn(first)
    for first, second in ((2, 1), (3, 0)):
        for g in both:
            g.send_ahead(False, first)
            g.send_behind(False, second)
    turn(3)
    turn(2)

    for c in range(4):
        rows.send_ahead(True, c)
        rows.send_behind(True, 3 - c)
    far = {}
    for first, second in ((0, 3), (1, 2)):
        for c in (first, second):
            turned[c].wait_recv()
            cols.send_ahead(True, c)
            cols.send_behind(True, c)
    share(0, True, WHOLE)
    for first, second in ((0, 3), (1, 2)):
        for g in both:
            g.far_from_behind[False, first].wait_recv()
            g.far_from_ahead[False, second].wait_recv()
    for span in (MIDDLE, UPPER):
        for g, target in ((rows, beside), (cols, across)):
            piece = g.piece(2, False, span)
            far[g, span] = copy(piece, piece, target)
    share(2, False, WHOLE)
    for first, second in ((2, 1), (3, 0)):
        for g in both:
            g.from_behind[False, first].wait_recv()
            g.from_ahead[False, second].wait_recv()
    share(3, False, WHOLE)
    share(1, False, WHOLE)
    for g in both:
        g.from_behind[True, 0].wait_recv()
        g.pass_ahead(True, 0, LOW)
        g.from_ahead[True, 3].wait_recv()
        g.pass_behind(True, 3, HIGH)
    wait_shared()
    multiply(0)

    for g in both:
        for c in (1, 2):
            g.from_behind[True, c].wait_recv()
            g.from_ahead[True, 3 - c].wait_recv()
        if g is cols:
            g.from_behind[True, 3].wait_recv()
            g.from_ahead[True, 0].wait_recv()
            share(3, True, WHOLE)
            share(1, True, WHOLE)
    rows.from_behind[True, 3].wait_recv()
    rows.from_ahead[True, 0].wait_recv()
    wait_shared()
    multiply(1)

    for span in (MIDDLE, UPPER):
        for g in both:
            far[g, span].wait_recv()
    share(2, True, (MIDDLE[0], UPPER[1]))
    cols.far_from_behind[True, 0].wait_recv()
    share(2, True, LOW)
    cols.far_from_ahead[True, 3].wait_recv()
    share(2, True, HIGH)
    rows.far_from_behind[True, 0].wait_recv()
    rows.far_from_ahead[True, 3].wait_recv()
    wait_shared()
    multiply(2)

    mask = spread(pats[2])
    for i in range(BLOCK_ROWS):
        block_rows = pl.ds(i * BLOCK, BLOCK)
        out[block_rows, :] = acc[block_rows, :] * mask[i : i + 1, :]
    for made in started:
        made.wait_send()


def shards(hamiltonian, density, h_pattern, p_pattern, keep_mask):
    return pl.pallas_call(
        kernel,
        out_shape=jax.ShapeDtypeStruct((ROWS, COLS), jnp.float32),
        in_specs=[pl.BlockSpec(memory_space=pl.ANY)] * 5,
        out_specs=pl.BlockSpec(memory_space=pltpu.VMEM),
        scratch_shapes=[
            pltpu.VMEM((8, 2, ROWS, COLS), jnp.bfloat16),
            pltpu.VMEM((8, 2, 2 * ROWS, COLS), jnp.bfloat16),
            pltpu.VMEM((ROWS, COLS), jnp.float32),
            pltpu.VMEM((2, ROWS, COLS), jnp.bfloat16),
            pltpu.VMEM((3, BLOCK_ROWS, BLOCK_COLS), jnp.int32),
            pltpu.SemaphoreType.DMA((COPIES,)),
            pltpu.SemaphoreType.DMA((COPIES,)),
            pltpu.SemaphoreType.DMA((5,)),
        ],
        compiler_params=pltpu.CompilerParams(
            collective_id=0, has_side_effects=True, vmem_limit_bytes=60 * 1024 * 1024
        ),
        name="commutator",
    )(hamiltonian, density, h_pattern, p_pattern, keep_mask)


def solution(mesh):
    return jax.shard_map(
        shards,
        mesh=mesh,
        in_specs=(
            P("row", "col"),
            P("row", "col"),
            P("row", "col"),
            P("row", "col"),
            P("row", "col"),
        ),
        out_specs=P("row", "col"),
        check_vma=False,
    )
```

```python
import jax
import jax.numpy as jnp
from jax import lax
from jax.experimental import pallas as pl
from jax.experimental.pallas import tpu as pltpu
from jax.sharding import PartitionSpec as P

MESH = pl.DeviceIdType.MESH
ROWS = 384
COLS = 768
BLOCK = 64
BLOCK_ROWS = ROWS // BLOCK
BLOCK_COLS = COLS // BLOCK
CUTS = (0, 128, 192, 256, 384)
CHUNKS = tuple(zip(CUTS[:-1], CUTS[1:]))
WHOLE = (0, ROWS)
LOW = (0, 64)
MIDDLE = (64, 192)
UPPER = (192, 320)
HIGH = (320, 384)
TAIL = 128
COPIES = 96


def device_of(x, y, z, core):
    return (4 * z + 2 * (y // 2) + core, 2 * x + y % 2)


def spread(pattern):
    block_of = lax.broadcasted_iota(jnp.int32, (BLOCK_COLS, COLS), 1) // BLOCK
    index = lax.broadcasted_iota(jnp.int32, (BLOCK_COLS, COLS), 0)
    select = jnp.where(block_of == index, 1.0, 0.0).astype(jnp.float32)
    return jnp.dot(pattern.astype(jnp.float32), select, preferred_element_type=jnp.float32)


class Gather:
    def __init__(self, copy, part, place, low, ahead, behind):
        self.copy, self.part, self.place, self.low = copy, part, place, low
        self.ahead, self.behind = ahead, behind
        self.from_behind, self.from_ahead = {}, {}
        self.far_from_behind, self.far_from_ahead = {}, {}

    def k(self, offset, other):
        low = 1 - self.low if other else self.low
        return 2 * ((self.place + offset) % 4) + low

    def piece(self, offset, other, span):
        return self.part(self.k(offset, other), *span)

    def send_ahead(self, other, c):
        piece = self.piece(0, other, CHUNKS[c])
        self.from_behind[other, c] = self.copy(piece, piece, self.ahead)

    def send_behind(self, other, c):
        piece = self.piece(0, other, CHUNKS[c])
        self.from_ahead[other, c] = self.copy(piece, piece, self.behind)

    def pass_ahead(self, other, c, span):
        piece = self.piece(3, other, span)
        self.far_from_behind[other, c] = self.copy(piece, piece, self.ahead)

    def pass_behind(self, other, c, span):
        piece = self.piece(1, other, span)
        self.far_from_ahead[other, c] = self.copy(piece, piece, self.behind)


def kernel(ham, den, h_pat, p_pat, keep, out, row, col, acc, tiles, pats, send, recv, load):
    row_index = lax.axis_index("row")
    col_index = lax.axis_index("col")
    x, y_lo = col_index // 2, col_index % 2
    z, y_hi, core = row_index // 4, (row_index // 2) % 2, row_index % 2
    y = 2 * y_hi + y_lo
    right = device_of((x + 1) % 4, y, z, core)
    left = device_of((x + 3) % 4, y, z, core)
    up = device_of(x, y, (z + 1) % 4, core)
    down = device_of(x, y, (z + 3) % 4, core)
    beside = device_of(x, 2 * y_hi + 1 - y_lo, z, core)
    across = device_of(x, 2 * (1 - y_hi) + y_lo, z, core)
    opposite = device_of(x, 3 - y, z, core)
    sibling = device_of(x, y, z, 1 - core)

    barrier = pltpu.get_barrier_semaphore()
    partners = (right, left, up, down, beside, across, opposite, sibling)
    for partner in partners:
        pl.semaphore_signal(barrier, inc=1, device_id=partner, device_id_type=MESH)

    loads = []
    pairs = (
        (h_pat, pats.at[0]),
        (ham, tiles.at[0]),
        (p_pat, pats.at[1]),
        (den, tiles.at[1]),
        (keep, pats.at[2]),
    )
    for i, (source, target) in enumerate(pairs):
        made = pltpu.make_async_copy(source, target, load.at[i])
        made.start()
        loads.append(made)

    row_own = 2 * x + y_lo
    col_own = 2 * z + y_hi
    base = core * ROWS
    for matrix in range(2):
        loads[2 * matrix].wait()
        loads[2 * matrix + 1].wait()
        mask = spread(pats[matrix]).astype(jnp.bfloat16)
        for i in range(BLOCK_ROWS):
            rows = pl.ds(i * BLOCK, BLOCK)
            masked = tiles[matrix, rows, :] * mask[i : i + 1, :]
            row[row_own, matrix, rows, :] = masked
            col[col_own, matrix, pl.ds(pl.multiple_of(base + i * BLOCK, BLOCK), BLOCK), :] = masked
    loads[4].wait()
    pl.semaphore_wait(barrier, len(partners))

    started = []

    def copy(source, landing, target):
        index = len(started)
        made = pltpu.make_async_remote_copy(
            src_ref=source,
            dst_ref=landing,
            send_sem=send.at[index],
            recv_sem=recv.at[index],
            device_id=target,
            device_id_type=MESH,
        )
        started.append(made)
        made.start()
        return made

    def row_part(k, first, last):
        return row.at[k, :, pl.ds(first, last - first), :]

    def col_part(k, first, last):
        start = pl.multiple_of(base + first, 16)
        return col.at[k, :, pl.ds(start, last - first), :]

    rows = Gather(copy, row_part, x, y_lo, right, left)
    cols = Gather(copy, col_part, z, y_hi, up, down)
    both = (rows, cols)
    shared = []

    def share(offset, other, span):
        piece = cols.piece(offset, other, span)
        shared.append(copy(piece, piece, sibling))

    def wait_shared():
        for made in shared:
            made.wait_recv()
        shared.clear()

    crossed, turned = {}, {}

    def cross(c):
        piece = rows.piece(0, False, CHUNKS[c])
        crossed[c] = copy(piece, piece, beside)

    def turn(c):
        crossed[c].wait_recv()
        landing = col_part(col_own, *CHUNKS[c])
        turned[c] = copy(rows.piece(0, True, CHUNKS[c]), landing, opposite)

    def kind_of(place, low, k):
        distance = (k // 2 - place + 4) % 4
        other = (k % 2 + low) % 2
        late = jnp.where(distance == 2, 2, 1)
        return jnp.where((other == 0) | (distance == 0), 0, late)

    def offset_of(place, k):
        behind = (k // 2 - place + 4) % 4 == 3
        return jnp.where(behind, 0, TAIL), jnp.where(behind, ROWS - TAIL, 0)

    def product(k, first, count, inner, depth):
        out_rows = pl.ds(pl.multiple_of(first, TAIL), count)

        def left(matrix):
            if depth == ROWS:
                return row[k, matrix, out_rows, :]
            spans = [pl.ds(pl.multiple_of(i * ROWS + inner, TAIL), depth) for i in range(2)]
            return jnp.concatenate([row[k, matrix, out_rows, span] for span in spans], axis=1)

        def right(matrix):
            if depth == ROWS:
                return col[k, matrix]
            spans = [pl.ds(pl.multiple_of(i * ROWS + inner, TAIL), depth) for i in range(2)]
            return jnp.concatenate([col[k, matrix, span, :] for span in spans], axis=0)

        forward = jnp.dot(left(0), right(1), preferred_element_type=jnp.float32)
        backward = jnp.dot(left(1), right(0), preferred_element_type=jnp.float32)
        acc[out_rows, :] += forward - backward

    def over_blocks(body):
        @pl.loop(0, 8)
        def _(k):
            body(k, kind_of(x, y_lo, k), kind_of(z, y_hi, k))

    def multiply_early(k, r, c):
        @pl.when((r == 0) & (c == 0))
        def _():
            product(k, 0, ROWS, 0, ROWS)

    def multiply_first(row_other, col_other):
        def body(k, r, c):
            row_start, _ = offset_of(x, k)
            col_start, _ = offset_of(z, k)

            @pl.when((r == 1) & (c == col_other))
            def _():
                product(k, row_start, ROWS - TAIL, 0, ROWS)

            @pl.when((r == row_other) & (c == 1))
            def _():
                product(k, 0, ROWS, col_start, ROWS - TAIL)

            if row_other == 0:

                @pl.when((r == 1) & (c == 1))
                def _():
                    product(k, row_start, ROWS - TAIL, col_start, ROWS - TAIL)

            else:

                @pl.when(((r == 2) & (c != 1)) | ((r != 1) & (c == 2)))
                def _():
                    product(k, 0, ROWS, 0, ROWS)

        return body

    def multiply_last_rows(k, r, c):
        _, row_start = offset_of(x, k)

        @pl.when((r == 1) & (c != 1))
        def _():
            product(k, row_start, TAIL, 0, ROWS)

    def multiply_last(k, r, c):
        row_first, row_start = offset_of(x, k)
        _, col_start = offset_of(z, k)

        @pl.when((r == 1) & (c == 1))
        def _():
            product(k, row_start, TAIL, 0, ROWS)
            product(k, row_first, ROWS - TAIL, col_start, TAIL)

        @pl.when((r != 1) & (c == 1))
        def _():
            product(k, 0, ROWS, col_start, TAIL)

    for first, second in ((0, 3), (1, 2)):
        for g in both:
            g.send_ahead(False, first)
            g.send_behind(False, second)
        cross(first)
        cross(second)
    share(0, False, WHOLE)
    acc[...] = jnp.zeros_like(acc)

    for first, second in ((0, 3), (1, 2)):
        for g in both:
            g.from_behind[False, first].wait_recv()
            g.pass_ahead(False, first, CHUNKS[first])
            g.from_ahead[False, second].wait_recv()
            g.pass_behind(False, second, CHUNKS[second])
        if first == 0:
            turn(0)
    for first, second in ((2, 1), (3, 0)):
        for g in both:
            g.send_ahead(False, first)
            g.send_behind(False, second)
    for c in (3, 1, 2):
        turn(c)

    for c in range(3):
        rows.send_ahead(True, c)
        rows.send_behind(True, 3 - c)
    far = {}
    for first, second in ((0, 3), (1, 2)):
        for g in both:
            g.far_from_behind[False, first].wait_recv()
            g.far_from_ahead[False, second].wait_recv()
    for span in (MIDDLE, UPPER):
        for g, target in ((rows, beside), (cols, across)):
            piece = g.piece(2, False, span)
            far[g, span] = copy(piece, piece, target)
    share(2, False, WHOLE)
    turned[0].wait_recv()
    cols.send_ahead(True, 0)
    turned[3].wait_recv()
    cols.send_behind(True, 3)
    turned[1].wait_recv()
    cols.send_ahead(True, 1)
    turned[2].wait_recv()
    cols.send_ahead(True, 2)
    cols.send_behind(True, 2)
    cols.send_behind(True, 1)
    share(0, True, WHOLE)
    for first, second in ((2, 1), (3, 0)):
        for g in both:
            g.from_behind[False, first].wait_recv()
            g.from_ahead[False, second].wait_recv()
    share(3, False, WHOLE)
    share(1, False, WHOLE)
    for g in both:
        g.from_behind[True, 0].wait_recv()
        g.pass_ahead(True, 0, LOW)
        g.send_ahead(True, 3)
        g.from_ahead[True, 3].wait_recv()
        g.pass_behind(True, 3, HIGH)
        g.send_behind(True, 0)
    wait_shared()
    over_blocks(multiply_early)

    for g in (cols, rows):
        for c in (1, 2):
            g.from_behind[True, c].wait_recv()
            g.from_ahead[True, 3 - c].wait_recv()
        if g is cols:
            share(3, True, (0, ROWS - TAIL))
            share(1, True, (TAIL, ROWS))
    wait_shared()
    over_blocks(multiply_first(0, 0))

    for span in (MIDDLE, UPPER):
        far[cols, span].wait_recv()
        share(2, True, span)
    cols.far_from_behind[True, 0].wait_recv()
    share(2, True, LOW)
    cols.far_from_ahead[True, 3].wait_recv()
    share(2, True, HIGH)
    for span in (MIDDLE, UPPER):
        far[rows, span].wait_recv()
    rows.far_from_behind[True, 0].wait_recv()
    rows.far_from_ahead[True, 3].wait_recv()
    wait_shared()
    over_blocks(multiply_first(2, 2))

    cols.from_behind[True, 3].wait_recv()
    share(3, True, CHUNKS[3])
    cols.from_ahead[True, 0].wait_recv()
    share(1, True, CHUNKS[0])
    rows.from_behind[True, 3].wait_recv()
    rows.from_ahead[True, 0].wait_recv()
    over_blocks(multiply_last_rows)
    wait_shared()
    over_blocks(multiply_last)

    mask = spread(pats[2])
    for i in range(BLOCK_ROWS):
        block_rows = pl.ds(i * BLOCK, BLOCK)
        out[block_rows, :] = acc[block_rows, :] * mask[i : i + 1, :]
    for made in started:
        made.wait_send()


def shards(hamiltonian, density, h_pattern, p_pattern, keep_mask):
    return pl.pallas_call(
        kernel,
        out_shape=jax.ShapeDtypeStruct((ROWS, COLS), jnp.float32),
        in_specs=[pl.BlockSpec(memory_space=pl.ANY)] * 5,
        out_specs=pl.BlockSpec(memory_space=pltpu.VMEM),
        scratch_shapes=[
            pltpu.VMEM((8, 2, ROWS, COLS), jnp.bfloat16),
            pltpu.VMEM((8, 2, 2 * ROWS, COLS), jnp.bfloat16),
            pltpu.VMEM((ROWS, COLS), jnp.float32),
            pltpu.VMEM((2, ROWS, COLS), jnp.bfloat16),
            pltpu.VMEM((3, BLOCK_ROWS, BLOCK_COLS), jnp.int32),
            pltpu.SemaphoreType.DMA((COPIES,)),
            pltpu.SemaphoreType.DMA((COPIES,)),
            pltpu.SemaphoreType.DMA((5,)),
        ],
        compiler_params=pltpu.CompilerParams(
            collective_id=0, has_side_effects=True, vmem_limit_bytes=60 * 1024 * 1024
        ),
        name="commutator",
    )(hamiltonian, density, h_pattern, p_pattern, keep_mask)


def solution(mesh):
    return jax.shard_map(
        shards,
        mesh=mesh,
        in_specs=(
            P("row", "col"),
            P("row", "col"),
            P("row", "col"),
            P("row", "col"),
            P("row", "col"),
        ),
        out_specs=P("row", "col"),
        check_vma=False,
    )
```

```python
import jax
import jax.numpy as jnp
from jax import lax
from jax.experimental import pallas as pl
from jax.experimental.pallas import tpu as pltpu
from jax.sharding import PartitionSpec as P

MESH = pl.DeviceIdType.MESH
ROWS = 384
COLS = 768
BLOCK = 64
BLOCK_ROWS = ROWS // BLOCK
BLOCK_COLS = COLS // BLOCK
CUTS = (0, 128, 192, 256, 384)
CHUNKS = tuple(zip(CUTS[:-1], CUTS[1:]))
WHOLE = (0, ROWS)
LOW = (0, 64)
MIDDLE = ((64, 128), (128, 192), (192, 256), (256, 320))
HIGH = (320, 384)
TAIL = 128
ARRIVALS = 38


def device_of(x, y, z, core):
    return (4 * z + 2 * (y // 2) + core, 2 * x + y % 2)


def spread(pattern):
    block_of = lax.broadcasted_iota(jnp.int32, (BLOCK_COLS, COLS), 1) // BLOCK
    index = lax.broadcasted_iota(jnp.int32, (BLOCK_COLS, COLS), 0)
    select = jnp.where(block_of == index, 1.0, 0.0).astype(jnp.float32)
    return jnp.dot(pattern.astype(jnp.float32), select, preferred_element_type=jnp.float32)


class Gather:
    def __init__(self, copy, arrival, part, place, low, ahead, behind):
        self.copy, self.part, self.place, self.low = copy, part, place, low
        self.ahead, self.behind = ahead, behind
        first, second, third, fourth, last = (arrival() for _ in range(5))
        self.from_behind = {(False, 0): first, (False, 1): second, (False, 2): last, (False, 3): last}
        self.from_ahead = {(False, 3): third, (False, 2): fourth, (False, 1): last, (False, 0): last}
        first, second, middle, last = (arrival() for _ in range(4))
        self.from_behind.update({(True, 0): first, (True, 1): middle, (True, 2): middle, (True, 3): last})
        self.from_ahead.update({(True, 3): second, (True, 2): middle, (True, 1): middle, (True, 0): last})
        outer, inner = arrival(), arrival()
        self.far = {0: outer, 3: outer, 1: inner, 2: inner}
        self.far_passed, self.far_crossed = arrival(), arrival()

    def k(self, offset, other):
        low = 1 - self.low if other else self.low
        return 2 * ((self.place + offset) % 4) + low

    def piece(self, offset, other, span):
        return self.part(self.k(offset, other), *span)

    def move(self, offset, other, span, target, arrival):
        piece = self.piece(offset, other, span)
        self.copy(piece, piece, target, span, arrival)

    def send_ahead(self, other, c):
        self.move(0, other, CHUNKS[c], self.ahead, self.from_behind[other, c])

    def send_behind(self, other, c):
        self.move(0, other, CHUNKS[c], self.behind, self.from_ahead[other, c])

    def pass_ahead(self, c):
        self.move(3, False, CHUNKS[c], self.ahead, self.far[c])

    def pass_behind(self, c):
        self.move(1, False, CHUNKS[c], self.behind, self.far[c])

    def pass_edges(self):
        self.from_behind[True, 0].wait()
        self.move(3, True, LOW, self.ahead, self.far_passed)
        self.send_ahead(True, 3)
        self.from_ahead[True, 3].wait()
        self.move(1, True, HIGH, self.behind, self.far_passed)
        self.send_behind(True, 0)

    def cross_far(self, c, target):
        self.move(2, False, MIDDLE[c], target, self.far_crossed)


def kernel(ham, den, h_pat, p_pat, keep, out, row, col, acc, tiles, pats, send, recv, load):
    row_index = lax.axis_index("row")
    col_index = lax.axis_index("col")
    x, y_lo = col_index // 2, col_index % 2
    z, y_hi, core = row_index // 4, (row_index // 2) % 2, row_index % 2
    y = 2 * y_hi + y_lo
    right = device_of((x + 1) % 4, y, z, core)
    left = device_of((x + 3) % 4, y, z, core)
    up = device_of(x, y, (z + 1) % 4, core)
    down = device_of(x, y, (z + 3) % 4, core)
    beside = device_of(x, 2 * y_hi + 1 - y_lo, z, core)
    across = device_of(x, 2 * (1 - y_hi) + y_lo, z, core)
    opposite = device_of(x, 3 - y, z, core)
    sibling = device_of(x, y, z, 1 - core)

    barrier = pltpu.get_barrier_semaphore()
    partners = (right, left, up, down, beside, across, opposite, sibling)
    for partner in partners:
        pl.semaphore_signal(barrier, inc=1, device_id=partner, device_id_type=MESH)

    loads = []
    pairs = (
        (h_pat, pats.at[0]),
        (ham, tiles.at[0]),
        (p_pat, pats.at[1]),
        (den, tiles.at[1]),
        (keep, pats.at[2]),
    )
    for i, (source, target) in enumerate(pairs):
        made = pltpu.make_async_copy(source, target, load.at[i])
        made.start()
        loads.append(made)

    row_own = 2 * x + y_lo
    col_own = 2 * z + y_hi
    base = core * ROWS
    for matrix in range(2):
        loads[2 * matrix].wait()
        loads[2 * matrix + 1].wait()
        mask = spread(pats[matrix]).astype(jnp.bfloat16)
        for i in range(BLOCK_ROWS):
            rows = pl.ds(i * BLOCK, BLOCK)
            masked = tiles[matrix, rows, :] * mask[i : i + 1, :]
            row[row_own, matrix, rows, :] = masked
            col[col_own, matrix, pl.ds(pl.multiple_of(base + i * BLOCK, BLOCK), BLOCK), :] = masked
    loads[4].wait()
    pl.semaphore_wait(barrier, len(partners))

    def extent(count):
        if count <= 2 * ROWS:
            return col.at[0, :, pl.ds(0, count), :]
        if count <= 8 * ROWS:
            return row.at[pl.ds(0, count // ROWS)]
        return col.at[pl.ds(0, count // (2 * ROWS))]

    def described(source, landing, target, sender, arrival):
        return pltpu.make_async_remote_copy(
            src_ref=source,
            dst_ref=landing,
            send_sem=send.at[sender],
            recv_sem=recv.at[arrival],
            device_id=target,
            device_id_type=MESH,
        )

    arrivals = []

    class Arrival:
        def __init__(self):
            self.index, self.count = len(arrivals), 0
            arrivals.append(self)

        def wait(self):
            if self.count:
                area = extent(self.count)
                described(area, area, sibling, 0, self.index).wait_recv()
                self.count = 0

    sent = [0, 0]

    def copier(sender):
        def copy(source, landing, target, span, arrival):
            arrival.count += span[1] - span[0]
            sent[sender] += span[1] - span[0]
            described(source, landing, target, sender, arrival.index).start()

        return copy

    copy_row, copy_col = copier(0), copier(1)

    def row_part(k, first, last):
        return row.at[k, :, pl.ds(first, last - first), :]

    def col_part(k, first, last):
        start = pl.multiple_of(base + first, 16)
        return col.at[k, :, pl.ds(start, last - first), :]

    rows = Gather(copy_row, Arrival, row_part, x, y_lo, right, left)
    cols = Gather(copy_col, Arrival, col_part, z, y_hi, up, down)
    both = (rows, cols)
    crossed = [Arrival() for _ in CHUNKS]
    turned = [Arrival() for _ in CHUNKS]
    shared = [Arrival() for _ in range(4)]

    def share(stage, offset, other, span):
        cols.move(offset, other, span, sibling, shared[stage])

    def cross(c):
        rows.move(0, False, CHUNKS[c], beside, crossed[c])

    def turn(c):
        crossed[c].wait()
        landing = col_part(col_own, *CHUNKS[c])
        copy_row(rows.piece(0, True, CHUNKS[c]), landing, opposite, CHUNKS[c], turned[c])

    def kind_of(place, low, k):
        distance = (k // 2 - place + 4) % 4
        other = (k % 2 + low) % 2
        late = jnp.where(distance == 2, 2, 1)
        return jnp.where((other == 0) | (distance == 0), 0, late)

    def offset_of(place, k):
        behind = (k // 2 - place + 4) % 4 == 3
        return jnp.where(behind, 0, TAIL), jnp.where(behind, ROWS - TAIL, 0)

    def product(k, first, count, inner, depth):
        out_rows = pl.ds(pl.multiple_of(first, TAIL), count)

        def left(matrix):
            if depth == ROWS:
                return row[k, matrix, out_rows, :]
            spans = [pl.ds(pl.multiple_of(i * ROWS + inner, TAIL), depth) for i in range(2)]
            return jnp.concatenate([row[k, matrix, out_rows, span] for span in spans], axis=1)

        def right(matrix):
            if depth == ROWS:
                return col[k, matrix]
            spans = [pl.ds(pl.multiple_of(i * ROWS + inner, TAIL), depth) for i in range(2)]
            return jnp.concatenate([col[k, matrix, span, :] for span in spans], axis=0)

        forward = jnp.dot(left(0), right(1), preferred_element_type=jnp.float32)
        backward = jnp.dot(left(1), right(0), preferred_element_type=jnp.float32)
        acc[out_rows, :] += forward - backward

    def over_blocks(body):
        @pl.loop(0, 8)
        def _(k):
            body(k, kind_of(x, y_lo, k), kind_of(z, y_hi, k))

    def multiply_early(k, r, c):
        @pl.when((r == 0) & (c == 0))
        def _():
            product(k, 0, ROWS, 0, ROWS)

    def multiply_first(row_other, col_other):
        def body(k, r, c):
            row_start, _ = offset_of(x, k)
            col_start, _ = offset_of(z, k)

            @pl.when((r == 1) & (c == col_other))
            def _():
                product(k, row_start, ROWS - TAIL, 0, ROWS)

            @pl.when((r == row_other) & (c == 1))
            def _():
                product(k, 0, ROWS, col_start, ROWS - TAIL)

            if row_other == 0:

                @pl.when((r == 1) & (c == 1))
                def _():
                    product(k, row_start, ROWS - TAIL, col_start, ROWS - TAIL)

            else:

                @pl.when(((r == 2) & (c != 1)) | ((r != 1) & (c == 2)))
                def _():
                    product(k, 0, ROWS, 0, ROWS)

        return body

    def multiply_last_rows(k, r, c):
        _, row_start = offset_of(x, k)

        @pl.when((r == 1) & (c != 1))
        def _():
            product(k, row_start, TAIL, 0, ROWS)

    def multiply_last(k, r, c):
        row_first, row_start = offset_of(x, k)
        _, col_start = offset_of(z, k)

        @pl.when((r == 1) & (c == 1))
        def _():
            product(k, row_start, TAIL, 0, ROWS)
            product(k, row_first, ROWS - TAIL, col_start, TAIL)

        @pl.when((r != 1) & (c == 1))
        def _():
            product(k, 0, ROWS, col_start, TAIL)

    for first, second in ((0, 3), (1, 2)):
        for g in both:
            g.send_ahead(False, first)
            g.send_behind(False, second)
        cross(first)
        cross(second)
    share(0, 0, False, WHOLE)
    acc[...] = jnp.zeros_like(acc)

    for first, second in ((0, 3), (1, 2)):
        for g in both:
            g.from_behind[False, first].wait()
            g.pass_ahead(first)
            g.from_ahead[False, second].wait()
            g.pass_behind(second)
        if first == 0:
            turn(0)
    for first, second in ((2, 1), (3, 0)):
        for g in both:
            g.send_ahead(False, first)
            g.send_behind(False, second)
    for c in (3, 1, 2):
        turn(c)

    for c in range(3):
        rows.send_ahead(True, c)
        rows.send_behind(True, 3 - c)
    for first, second in ((0, 3), (1, 2)):
        for g, target in ((rows, beside), (cols, across)):
            g.far[first].wait()
            g.cross_far(first, target)
            g.cross_far(second, target)
    share(0, 2, False, WHOLE)
    turned[0].wait()
    cols.send_ahead(True, 0)
    turned[3].wait()
    cols.send_behind(True, 3)
    turned[1].wait()
    cols.send_ahead(True, 1)
    turned[2].wait()
    cols.send_ahead(True, 2)
    cols.send_behind(True, 2)
    cols.send_behind(True, 1)
    share(0, 0, True, WHOLE)
    for g in both:
        g.from_behind[False, 3].wait()
    share(0, 3, False, WHOLE)
    share(0, 1, False, WHOLE)
    for g in both:
        g.pass_edges()
    shared[0].wait()
    over_blocks(multiply_early)

    cols.from_behind[True, 1].wait()
    share(1, 3, True, (0, ROWS - TAIL))
    share(1, 1, True, (TAIL, ROWS))
    rows.from_behind[True, 1].wait()
    shared[1].wait()
    over_blocks(multiply_first(0, 0))

    cols.far_crossed.wait()
    share(2, 2, True, (LOW[1], HIGH[0]))
    cols.far_passed.wait()
    share(2, 2, True, LOW)
    share(2, 2, True, HIGH)
    rows.far_crossed.wait()
    rows.far_passed.wait()
    shared[2].wait()
    over_blocks(multiply_first(2, 2))

    cols.from_behind[True, 3].wait()
    share(3, 3, True, CHUNKS[3])
    share(3, 1, True, CHUNKS[0])
    rows.from_behind[True, 3].wait()
    over_blocks(multiply_last_rows)
    shared[3].wait()
    over_blocks(multiply_last)

    mask = spread(pats[2])
    for i in range(BLOCK_ROWS):
        block_rows = pl.ds(i * BLOCK, BLOCK)
        out[block_rows, :] = acc[block_rows, :] * mask[i : i + 1, :]
    for sender, count in enumerate(sent):
        area = extent(count)
        described(area, area, sibling, sender, 0).wait_send()


def shards(*arrays):
    arrays = [pltpu.with_memory_space_constraint(array, pltpu.HBM) for array in arrays]
    return pl.pallas_call(
        kernel,
        out_shape=jax.ShapeDtypeStruct((ROWS, COLS), jnp.float32),
        in_specs=[pl.BlockSpec(memory_space=pl.ANY)] * 5,
        out_specs=pl.BlockSpec(memory_space=pltpu.VMEM),
        scratch_shapes=[
            pltpu.VMEM((8, 2, ROWS, COLS), jnp.bfloat16),
            pltpu.VMEM((8, 2, 2 * ROWS, COLS), jnp.bfloat16),
            pltpu.VMEM((ROWS, COLS), jnp.float32),
            pltpu.VMEM((2, ROWS, COLS), jnp.bfloat16),
            pltpu.VMEM((3, BLOCK_ROWS, BLOCK_COLS), jnp.int32),
            pltpu.SemaphoreType.DMA((2,)),
            pltpu.SemaphoreType.DMA((ARRIVALS,)),
            pltpu.SemaphoreType.DMA((5,)),
        ],
        compiler_params=pltpu.CompilerParams(
            collective_id=0, has_side_effects=True, vmem_limit_bytes=48 * 1024 * 1024
        ),
        name="commutator",
    )(*arrays)


def solution(mesh):
    return jax.shard_map(
        shards,
        mesh=mesh,
        in_specs=(
            P("row", "col"),
            P("row", "col"),
            P("row", "col"),
            P("row", "col"),
            P("row", "col"),
        ),
        out_specs=P("row", "col"),
        check_vma=False,
    )
```

```python
import functools

import jax
import jax.numpy as jnp
from jax import lax
from jax.experimental import pallas as pl
from jax.experimental.pallas import tpu as pltpu
from jax.sharding import PartitionSpec as P

MESH = pl.DeviceIdType.MESH
ROWS = 384
COLS = 768
BLOCK = 64
BLOCK_ROWS = ROWS // BLOCK
BLOCK_COLS = COLS // BLOCK
CUTS = (0, 128, 192, 256, 384)
CHUNKS = tuple(zip(CUTS[:-1], CUTS[1:]))
WHOLE = (0, ROWS)
EDGE = 48
LOW_EDGE = (ROWS - 2 * EDGE, ROWS - EDGE)
HIGH_EDGE = (ROWS - EDGE, ROWS)
TAIL = 128
ARRIVALS = 39


def device_of(x, y, z, core):
    return (4 * z + 2 * (y // 2) + core, 2 * x + y % 2)


def spread(pattern):
    block_of = lax.broadcasted_iota(jnp.int32, (BLOCK_COLS, COLS), 1) // BLOCK
    index = lax.broadcasted_iota(jnp.int32, (BLOCK_COLS, COLS), 0)
    select = jnp.where(block_of == index, 1.0, 0.0).astype(jnp.float32)
    return jnp.dot(pattern.astype(jnp.float32), select, preferred_element_type=jnp.float32)


class Gather:
    def __init__(self, copy, arrival, part, place, low, ahead, behind, crossed):
        self.copy, self.part, self.place, self.low = copy, part, place, low
        self.ahead, self.behind, self.crossed = ahead, behind, crossed
        first, second, third, fourth, last = (arrival() for _ in range(5))
        self.from_behind = {(False, 0): first, (False, 1): second, (False, 2): last, (False, 3): last}
        self.from_ahead = {(False, 3): third, (False, 2): fourth, (False, 1): last, (False, 0): last}
        first, second, middle, last = (arrival() for _ in range(4))
        self.from_behind.update({(True, 3): first, (True, 1): middle, (True, 2): middle, (True, 0): last})
        self.from_ahead.update({(True, 3): second, (True, 1): middle, (True, 2): middle, (True, 0): last})
        outer, inner = arrival(), arrival()
        self.far = {0: outer, 3: outer, 1: inner, 2: inner}
        self.far_crossed, self.far_edges = arrival(), arrival()

    def k(self, offset, other):
        low = 1 - self.low if other else self.low
        return 2 * ((self.place + offset) % 4) + low

    def piece(self, offset, other, span):
        return self.part(self.k(offset, other), *span)

    def move(self, offset, other, span, target, arrival):
        piece = self.piece(offset, other, span)
        self.copy(piece, piece, target, span, arrival)

    def send_ahead(self, other, c):
        self.move(0, other, CHUNKS[c], self.ahead, self.from_behind[other, c])

    def send_behind(self, other, c):
        self.move(0, other, CHUNKS[c], self.behind, self.from_ahead[other, c])

    def pass_ahead(self, c):
        self.move(3, False, CHUNKS[c], self.ahead, self.far[c])

    def pass_behind(self, c):
        self.move(1, False, CHUNKS[c], self.behind, self.far[c])

    def pass_edges(self):
        self.from_behind[True, 3].wait()
        self.move(3, True, LOW_EDGE, self.ahead, self.far_edges)
        self.from_ahead[True, 3].wait()
        self.move(1, True, HIGH_EDGE, self.behind, self.far_edges)

    def cross_far(self, c, target):
        span = (CHUNKS[c][0], min(CHUNKS[c][1], LOW_EDGE[0]))
        arrival = self.far_crossed if c in self.crossed else self.far_edges
        self.move(2, False, span, target, arrival)


def kernel(ham, den, h_pat, p_pat, keep, out, row, col, acc, tiles, pats, send, recv, load):
    row_index = lax.axis_index("row")
    col_index = lax.axis_index("col")
    x, y_lo = col_index // 2, col_index % 2
    z, y_hi, core = row_index // 4, (row_index // 2) % 2, row_index % 2
    y = 2 * y_hi + y_lo
    right = device_of((x + 1) % 4, y, z, core)
    left = device_of((x + 3) % 4, y, z, core)
    up = device_of(x, y, (z + 1) % 4, core)
    down = device_of(x, y, (z + 3) % 4, core)
    beside = device_of(x, 2 * y_hi + 1 - y_lo, z, core)
    across = device_of(x, 2 * (1 - y_hi) + y_lo, z, core)
    opposite = device_of(x, 3 - y, z, core)
    sibling = device_of(x, y, z, 1 - core)

    barrier = pltpu.get_barrier_semaphore()
    partners = (right, left, up, down, beside, across, opposite, sibling)
    for partner in partners:
        pl.semaphore_signal(barrier, inc=1, device_id=partner, device_id_type=MESH)

    loads = []
    pairs = (
        (h_pat, pats.at[0]),
        (ham, tiles.at[0]),
        (p_pat, pats.at[1]),
        (den, tiles.at[1]),
        (keep, pats.at[2]),
    )
    for i, (source, target) in enumerate(pairs):
        made = pltpu.make_async_copy(source, target, load.at[i])
        made.start()
        loads.append(made)

    row_own = 2 * x + y_lo
    col_own = 2 * z + y_hi
    base = core * ROWS
    for matrix in range(2):
        loads[2 * matrix].wait()
        loads[2 * matrix + 1].wait()
        mask = spread(pats[matrix]).astype(jnp.bfloat16)
        for i in range(BLOCK_ROWS):
            rows = pl.ds(i * BLOCK, BLOCK)
            masked = tiles[matrix, rows, :] * mask[i : i + 1, :]
            row[row_own, matrix, rows, :] = masked
            col[col_own, matrix, pl.ds(pl.multiple_of(base + i * BLOCK, BLOCK), BLOCK), :] = masked
    loads[4].wait()
    pl.semaphore_wait(barrier, len(partners))

    def extent(count):
        if count <= 2 * ROWS:
            return col.at[0, :, pl.ds(0, count), :]
        if count <= 8 * ROWS:
            return row.at[pl.ds(0, count // ROWS)]
        return col.at[pl.ds(0, count // (2 * ROWS))]

    def described(source, landing, target, sender, arrival):
        return pltpu.make_async_remote_copy(
            src_ref=source,
            dst_ref=landing,
            send_sem=send.at[sender],
            recv_sem=recv.at[arrival],
            device_id=target,
            device_id_type=MESH,
        )

    arrivals = []

    class Arrival:
        def __init__(self):
            self.index, self.count = len(arrivals), 0
            arrivals.append(self)

        def wait(self):
            if self.count:
                area = extent(self.count)
                described(area, area, sibling, 0, self.index).wait_recv()
                self.count = 0

    sent = [0, 0]

    def copier(sender):
        def copy(source, landing, target, span, arrival):
            arrival.count += span[1] - span[0]
            sent[sender] += span[1] - span[0]
            described(source, landing, target, sender, arrival.index).start()

        return copy

    copy_row, copy_col = copier(0), copier(1)

    def row_part(k, first, last):
        return row.at[k, :, pl.ds(first, last - first), :]

    def col_part(k, first, last):
        start = pl.multiple_of(base + first, 16)
        return col.at[k, :, pl.ds(start, last - first), :]

    rows = Gather(copy_row, Arrival, row_part, x, y_lo, right, left, (0, 1, 2))
    cols = Gather(copy_col, Arrival, col_part, z, y_hi, up, down, (0,))
    both = (rows, cols)
    crossed = [Arrival() for _ in CHUNKS]
    turned = [Arrival() for _ in CHUNKS]
    shared = [Arrival() for _ in range(5)]

    def share(stage, offset, other, span):
        cols.move(offset, other, span, sibling, shared[stage])

    def cross(c):
        rows.move(0, False, CHUNKS[c], beside, crossed[c])

    def turn(c):
        crossed[c].wait()
        landing = col_part(col_own, *CHUNKS[c])
        copy_row(rows.piece(0, True, CHUNKS[c]), landing, opposite, CHUNKS[c], turned[c])

    def kind_of(place, low, k):
        distance = (k // 2 - place + 4) % 4
        other = (k % 2 + low) % 2
        late = jnp.where(distance == 2, 2, 1)
        return jnp.where((other == 0) | (distance == 0), 0, late)

    def product(k, out_part, inner_part):
        out_span = slice(*out_part)
        if inner_part == WHOLE:
            inner_spans = [slice(None)]
        else:
            inner_spans = [slice(base + inner_part[0], base + inner_part[1]) for base in (0, ROWS)]

        def left(matrix):
            pieces = [row[k, matrix, out_span, inner] for inner in inner_spans]
            return jnp.concatenate(pieces, axis=1)

        def right(matrix):
            return jnp.concatenate([col[k, matrix, inner, :] for inner in inner_spans], axis=0)

        forward = jnp.dot(left(0), right(1), preferred_element_type=jnp.float32)
        backward = jnp.dot(left(1), right(0), preferred_element_type=jnp.float32)
        acc[out_span, :] += forward - backward

    def stage(*entries):
        @pl.loop(0, 8)
        def _(k):
            r, c = kind_of(x, y_lo, k), kind_of(z, y_hi, k)
            for row_kinds, col_kinds, *parts in entries:
                row_fits = functools.reduce(jnp.logical_or, [r == kind for kind in row_kinds])
                col_fits = functools.reduce(jnp.logical_or, [c == kind for kind in col_kinds])

                @pl.when(row_fits & col_fits)
                def _():
                    for out_part, inner_part in parts:
                        product(k, out_part, inner_part)

    near_first, near_last = (TAIL, ROWS), (0, TAIL)
    far_rows_first, far_rows_last = (0, 2 * TAIL), (2 * TAIL, ROWS)
    far_cols_first, far_cols_last = (0, TAIL), (TAIL, ROWS)

    for first, second in ((0, 3), (1, 2)):
        for g in both:
            g.send_ahead(False, first)
            g.send_behind(False, second)
        if first == 0:
            cross(3)
            cross(1)
    cross(2)
    cross(0)
    share(0, 0, False, WHOLE)
    acc[...] = jnp.zeros_like(acc)

    for first, second in ((0, 3), (1, 2)):
        for g in both:
            g.from_behind[False, first].wait()
            g.pass_ahead(first)
            g.from_ahead[False, second].wait()
            g.pass_behind(second)
        if first == 0:
            turn(3)
    for first, second in ((2, 1), (3, 0)):
        for g in both:
            g.send_ahead(False, first)
            g.send_behind(False, second)
    turn(1)
    turn(2)

    def cross_far(g, target, *chunks):
        for c in chunks:
            g.far[c].wait()
            g.cross_far(c, target)

    cross_far(rows, beside, 0)
    turn(0)
    for c in (3, 1, 2, 0):
        rows.send_ahead(True, c)
        rows.send_behind(True, c)
    cross_far(rows, beside, 1, 2, 3)
    for c in (3, 1, 2, 0):
        turned[c].wait()
        cols.send_ahead(True, c)
        cols.send_behind(True, c)
    share(0, 0, True, WHOLE)
    cross_far(cols, across, 0, 1, 2, 3)
    share(0, 2, False, WHOLE)
    for g in both:
        g.from_behind[False, 3].wait()
    share(0, 3, False, WHOLE)
    share(0, 1, False, WHOLE)
    for g in both:
        g.pass_edges()
    shared[0].wait()
    stage(((0,), (0,), (WHOLE, WHOLE)))

    rows.far_crossed.wait()
    stage(((2,), (0,), (far_rows_first, WHOLE)))

    cols.from_behind[True, 1].wait()
    share(1, 3, True, near_first)
    share(1, 1, True, near_first)
    cols.far_crossed.wait()
    share(2, 2, True, far_cols_first)
    rows.from_behind[True, 1].wait()
    shared[1].wait()
    shared[2].wait()
    stage(
        ((1,), (0,), (near_first, WHOLE)),
        ((0,), (1,), (WHOLE, near_first)),
        ((1,), (1,), (near_first, near_first)),
        ((2,), (1,), (far_rows_first, near_first)),
        ((0,), (2,), (WHOLE, far_cols_first)),
        ((1,), (2,), (near_first, far_cols_first)),
        ((2,), (2,), (far_rows_first, far_cols_first)),
    )

    cols.from_behind[True, 0].wait()
    share(3, 3, True, near_last)
    share(3, 1, True, near_last)
    rows.from_behind[True, 0].wait()
    stage(
        ((1,), (0,), (near_last, WHOLE)),
        ((1,), (2,), (near_last, far_cols_first)),
    )
    shared[3].wait()
    stage(
        ((0,), (1,), (WHOLE, near_last)),
        ((1,), (1,), (near_last, WHOLE), (near_first, near_last)),
        ((2,), (1,), (far_rows_first, near_last)),
    )

    cols.far_edges.wait()
    share(4, 2, True, far_cols_last)
    rows.far_edges.wait()
    stage(((2,), (0, 1), (far_rows_last, WHOLE)))
    shared[4].wait()
    stage(
        ((0, 1), (2,), (WHOLE, far_cols_last)),
        ((2,), (2,), (far_rows_last, WHOLE), (far_rows_first, far_cols_last)),
    )

    mask = spread(pats[2])
    for i in range(BLOCK_ROWS):
        block_rows = pl.ds(i * BLOCK, BLOCK)
        out[block_rows, :] = acc[block_rows, :] * mask[i : i + 1, :]
    for sender, count in enumerate(sent):
        area = extent(count)
        described(area, area, sibling, sender, 0).wait_send()


def shards(*arrays):
    arrays = [pltpu.with_memory_space_constraint(array, pltpu.HBM) for array in arrays]
    return pl.pallas_call(
        kernel,
        out_shape=jax.ShapeDtypeStruct((ROWS, COLS), jnp.float32),
        in_specs=[pl.BlockSpec(memory_space=pl.ANY)] * 5,
        out_specs=pl.BlockSpec(memory_space=pltpu.VMEM),
        scratch_shapes=[
            pltpu.VMEM((8, 2, ROWS, COLS), jnp.bfloat16),
            pltpu.VMEM((8, 2, 2 * ROWS, COLS), jnp.bfloat16),
            pltpu.VMEM((ROWS, COLS), jnp.float32),
            pltpu.VMEM((2, ROWS, COLS), jnp.bfloat16),
            pltpu.VMEM((3, BLOCK_ROWS, BLOCK_COLS), jnp.int32),
            pltpu.SemaphoreType.DMA((2,)),
            pltpu.SemaphoreType.DMA((ARRIVALS,)),
            pltpu.SemaphoreType.DMA((5,)),
        ],
        compiler_params=pltpu.CompilerParams(
            collective_id=0, has_side_effects=True, vmem_limit_bytes=48 * 1024 * 1024
        ),
        name="commutator",
    )(*arrays)


def solution(mesh):
    return jax.shard_map(
        shards,
        mesh=mesh,
        in_specs=(
            P("row", "col"),
            P("row", "col"),
            P("row", "col"),
            P("row", "col"),
            P("row", "col"),
        ),
        out_specs=P("row", "col"),
        check_vma=False,
    )
```

```python
import functools

import jax
import jax.numpy as jnp
from jax import lax
from jax.experimental import pallas as pl
from jax.experimental.pallas import tpu as pltpu
from jax.sharding import PartitionSpec as P

MESH = pl.DeviceIdType.MESH
ROWS = 384
COLS = 768
BLOCK = 64
BLOCK_ROWS = ROWS // BLOCK
BLOCK_COLS = COLS // BLOCK
CUTS = (0, 128, 192, 256, 384)
CHUNKS = tuple(zip(CUTS[:-1], CUTS[1:]))
WHOLE = (0, ROWS)
ROW_EDGE = 64
COL_EDGE = 32
TAIL = 128
ARRIVALS = 39


def device_of(x, y, z, core):
    return (4 * z + 2 * (y // 2) + core, 2 * x + y % 2)


def spread(pattern):
    block_of = lax.broadcasted_iota(jnp.int32, (BLOCK_COLS, COLS), 1) // BLOCK
    index = lax.broadcasted_iota(jnp.int32, (BLOCK_COLS, COLS), 0)
    select = jnp.where(block_of == index, 1.0, 0.0).astype(jnp.float32)
    return jnp.dot(pattern.astype(jnp.float32), select, preferred_element_type=jnp.float32)


class Gather:
    def __init__(self, copy, arrival, part, place, low, ahead, behind, crossed, edge):
        self.copy, self.part, self.place, self.low = copy, part, place, low
        self.ahead, self.behind, self.crossed = ahead, behind, crossed
        self.low_edge = (ROWS - 2 * edge, ROWS - edge)
        self.high_edge = (ROWS - edge, ROWS)
        first, second, third, fourth, last = (arrival() for _ in range(5))
        self.from_behind = {(False, 0): first, (False, 1): second, (False, 2): last, (False, 3): last}
        self.from_ahead = {(False, 3): third, (False, 2): fourth, (False, 1): last, (False, 0): last}
        first, second, middle, last = (arrival() for _ in range(4))
        self.from_behind.update({(True, 3): first, (True, 1): middle, (True, 2): middle, (True, 0): last})
        self.from_ahead.update({(True, 3): second, (True, 1): middle, (True, 2): middle, (True, 0): last})
        outer, inner = arrival(), arrival()
        self.far = {0: outer, 3: outer, 1: inner, 2: inner}
        self.far_crossed, self.far_edges = arrival(), arrival()

    def k(self, offset, other):
        low = 1 - self.low if other else self.low
        return 2 * ((self.place + offset) % 4) + low

    def piece(self, offset, other, span):
        return self.part(self.k(offset, other), *span)

    def move(self, offset, other, span, target, arrival):
        piece = self.piece(offset, other, span)
        self.copy(piece, piece, target, span, arrival)

    def send_ahead(self, other, c):
        self.move(0, other, CHUNKS[c], self.ahead, self.from_behind[other, c])

    def send_behind(self, other, c):
        self.move(0, other, CHUNKS[c], self.behind, self.from_ahead[other, c])

    def pass_ahead(self, c):
        self.move(3, False, CHUNKS[c], self.ahead, self.far[c])

    def pass_behind(self, c):
        self.move(1, False, CHUNKS[c], self.behind, self.far[c])

    def pass_edges(self):
        self.from_behind[True, 3].wait()
        self.move(3, True, self.low_edge, self.ahead, self.far_edges)
        self.from_ahead[True, 3].wait()
        self.move(1, True, self.high_edge, self.behind, self.far_edges)

    def cross_far(self, c, target):
        span = (CHUNKS[c][0], min(CHUNKS[c][1], self.low_edge[0]))
        if span[0] == span[1]:
            return
        arrival = self.far_crossed if c in self.crossed else self.far_edges
        self.move(2, False, span, target, arrival)


def kernel(ham, den, h_pat, p_pat, keep, out, row, col, acc, kept, tiles, pats, send, recv, load):
    row_index = lax.axis_index("row")
    col_index = lax.axis_index("col")
    x, y_lo = col_index // 2, col_index % 2
    z, y_hi, core = row_index // 4, (row_index // 2) % 2, row_index % 2
    y = 2 * y_hi + y_lo
    right = device_of((x + 1) % 4, y, z, core)
    left = device_of((x + 3) % 4, y, z, core)
    up = device_of(x, y, (z + 1) % 4, core)
    down = device_of(x, y, (z + 3) % 4, core)
    beside = device_of(x, 2 * y_hi + 1 - y_lo, z, core)
    across = device_of(x, 2 * (1 - y_hi) + y_lo, z, core)
    opposite = device_of(x, 3 - y, z, core)
    sibling = device_of(x, y, z, 1 - core)

    barrier = pltpu.get_barrier_semaphore()
    partners = (right, left, up, down, beside, across, opposite, sibling)
    for partner in partners:
        pl.semaphore_signal(barrier, inc=1, device_id=partner, device_id_type=MESH)

    loads = []
    pairs = (
        (h_pat, pats.at[0]),
        (ham, tiles.at[0]),
        (p_pat, pats.at[1]),
        (den, tiles.at[1]),
        (keep, pats.at[2]),
    )
    for i, (source, target) in enumerate(pairs):
        made = pltpu.make_async_copy(source, target, load.at[i])
        made.start()
        loads.append(made)

    row_own = 2 * x + y_lo
    col_own = 2 * z + y_hi
    base = core * ROWS
    for matrix in range(2):
        loads[2 * matrix].wait()
        loads[2 * matrix + 1].wait()
        mask = spread(pats[matrix]).astype(jnp.bfloat16)
        for i in range(BLOCK_ROWS):
            rows = pl.ds(i * BLOCK, BLOCK)
            masked = tiles[matrix, rows, :] * mask[i : i + 1, :]
            row[row_own, matrix, rows, :] = masked
            col[col_own, matrix, pl.ds(pl.multiple_of(base + i * BLOCK, BLOCK), BLOCK), :] = masked
    loads[4].wait()
    pl.semaphore_wait(barrier, len(partners))

    def extent(count):
        if count <= 2 * ROWS:
            return col.at[0, :, pl.ds(0, count), :]
        if count <= 8 * ROWS:
            return row.at[pl.ds(0, count // ROWS)]
        return col.at[pl.ds(0, count // (2 * ROWS))]

    def described(source, landing, target, sender, arrival):
        return pltpu.make_async_remote_copy(
            src_ref=source,
            dst_ref=landing,
            send_sem=send.at[sender],
            recv_sem=recv.at[arrival],
            device_id=target,
            device_id_type=MESH,
        )

    arrivals = []

    class Arrival:
        def __init__(self):
            self.index, self.count = len(arrivals), 0
            arrivals.append(self)

        def wait(self):
            if self.count:
                area = extent(self.count)
                described(area, area, sibling, 0, self.index).wait_recv()
                self.count = 0

    sent = [0, 0]

    def copier(sender):
        def copy(source, landing, target, span, arrival):
            arrival.count += span[1] - span[0]
            sent[sender] += span[1] - span[0]
            described(source, landing, target, sender, arrival.index).start()

        return copy

    copy_row, copy_col = copier(0), copier(1)

    def row_part(k, first, last):
        return row.at[k, :, pl.ds(first, last - first), :]

    def col_part(k, first, last):
        start = pl.multiple_of(base + first, 16)
        return col.at[k, :, pl.ds(start, last - first), :]

    rows = Gather(copy_row, Arrival, row_part, x, y_lo, right, left, (0, 1, 2), ROW_EDGE)
    cols = Gather(copy_col, Arrival, col_part, z, y_hi, up, down, (0,), COL_EDGE)
    both = (rows, cols)
    crossed = [Arrival() for _ in CHUNKS]
    turned = [Arrival() for _ in CHUNKS]
    shared = [Arrival() for _ in range(5)]

    def share(stage, offset, other, span):
        cols.move(offset, other, span, sibling, shared[stage])

    def cross(c):
        rows.move(0, False, CHUNKS[c], beside, crossed[c])

    def turn(c):
        crossed[c].wait()
        landing = col_part(col_own, *CHUNKS[c])
        copy_row(rows.piece(0, True, CHUNKS[c]), landing, opposite, CHUNKS[c], turned[c])

    def kind_of(place, low, k):
        distance = (k // 2 - place + 4) % 4
        other = (k % 2 + low) % 2
        late = jnp.where(distance == 2, 2, 1)
        return jnp.where((other == 0) | (distance == 0), 0, late)

    def product(k, out_part, inner_part):
        out_span = slice(*out_part)
        if inner_part == WHOLE:
            inner_spans = [slice(None)]
        else:
            inner_spans = [slice(base + inner_part[0], base + inner_part[1]) for base in (0, ROWS)]

        def left(matrix):
            pieces = [row[k, matrix, out_span, inner] for inner in inner_spans]
            return jnp.concatenate(pieces, axis=1)

        def right(matrix):
            return jnp.concatenate([col[k, matrix, inner, :] for inner in inner_spans], axis=0)

        forward = jnp.dot(left(0), right(1), preferred_element_type=jnp.float32)
        backward = jnp.dot(left(1), right(0), preferred_element_type=jnp.float32)
        acc[out_span, :] += forward - backward

    def stage(*entries):
        @pl.loop(0, 8)
        def _(k):
            r, c = kind_of(x, y_lo, k), kind_of(z, y_hi, k)
            for row_kinds, col_kinds, *parts in entries:
                row_fits = functools.reduce(jnp.logical_or, [r == kind for kind in row_kinds])
                col_fits = functools.reduce(jnp.logical_or, [c == kind for kind in col_kinds])

                @pl.when(row_fits & col_fits)
                def _():
                    for out_part, inner_part in parts:
                        product(k, out_part, inner_part)

    near_first, near_last = (TAIL, ROWS), (0, TAIL)
    far_rows_first, far_rows_last = (0, 2 * TAIL), (2 * TAIL, ROWS)
    far_cols_first, far_cols_last = (0, TAIL), (TAIL, ROWS)

    for first, second in ((0, 3), (1, 2)):
        for g in both:
            g.send_ahead(False, first)
            g.send_behind(False, second)
        if first == 0:
            cross(3)
            cross(1)
    cross(2)
    cross(0)
    share(0, 0, False, WHOLE)
    acc[...] = jnp.zeros_like(acc)
    kept[...] = spread(pats[2])

    for first, second in ((0, 3), (1, 2)):
        for g in both:
            g.from_behind[False, first].wait()
            g.pass_ahead(first)
            g.from_ahead[False, second].wait()
            g.pass_behind(second)
        if first == 0:
            turn(3)
    for first, second in ((2, 1), (3, 0)):
        for g in both:
            g.send_ahead(False, first)
            g.send_behind(False, second)
    turn(1)
    turn(2)

    def cross_far(g, target, *chunks):
        for c in chunks:
            g.far[c].wait()
            g.cross_far(c, target)

    cross_far(rows, beside, 0)
    turn(0)
    for c in (3, 1, 2):
        rows.send_ahead(True, c)
        rows.send_behind(True, c)
    cross_far(rows, beside, 1, 2, 3)
    for c in (3, 1, 2, 0):
        turned[c].wait()
        cols.send_ahead(True, c)
        cols.send_behind(True, c)
    share(0, 0, True, WHOLE)
    cross_far(cols, across, 0, 1, 2, 3)
    share(0, 2, False, WHOLE)
    for g in both:
        g.from_behind[False, 3].wait()
    share(0, 3, False, WHOLE)
    share(0, 1, False, WHOLE)
    rows.pass_edges()
    rows.send_ahead(True, 0)
    rows.send_behind(True, 0)
    cols.pass_edges()
    shared[0].wait()
    stage(((0,), (0,), (WHOLE, WHOLE)))

    rows.far_crossed.wait()
    stage(((2,), (0,), (far_rows_first, WHOLE)))

    cols.from_behind[True, 1].wait()
    share(1, 3, True, near_first)
    share(1, 1, True, near_first)
    cols.far_crossed.wait()
    share(2, 2, True, far_cols_first)
    rows.from_behind[True, 1].wait()
    shared[1].wait()
    shared[2].wait()
    stage(
        ((1,), (0,), (near_first, WHOLE)),
        ((0,), (1,), (WHOLE, near_first)),
        ((1,), (1,), (near_first, near_first)),
        ((2,), (1,), (far_rows_first, near_first)),
        ((0,), (2,), (WHOLE, far_cols_first)),
        ((1,), (2,), (near_first, far_cols_first)),
        ((2,), (2,), (far_rows_first, far_cols_first)),
    )

    rows.far_edges.wait()
    stage(
        ((2,), (0,), (far_rows_last, WHOLE)),
        ((2,), (1,), (far_rows_last, near_first)),
        ((2,), (2,), (far_rows_last, far_cols_first)),
    )

    cols.from_behind[True, 0].wait()
    share(3, 3, True, near_last)
    share(3, 1, True, near_last)
    shared[3].wait()
    stage(
        ((0, 2), (1,), (WHOLE, near_last)),
        ((1,), (1,), (near_first, near_last)),
    )

    cols.far_edges.wait()
    share(4, 2, True, far_cols_last)
    rows.from_behind[True, 0].wait()
    stage(
        ((1,), (0, 1), (near_last, WHOLE)),
        ((1,), (2,), (near_last, far_cols_first)),
    )
    shared[4].wait()
    stage(((0, 1, 2), (2,), (WHOLE, far_cols_last)))

    for i in range(BLOCK_ROWS):
        block_rows = pl.ds(i * BLOCK, BLOCK)
        out[block_rows, :] = acc[block_rows, :] * kept[i : i + 1, :]
    for sender, count in enumerate(sent):
        area = extent(count)
        described(area, area, sibling, sender, 0).wait_send()


def shards(*arrays):
    arrays = [pltpu.with_memory_space_constraint(array, pltpu.HBM) for array in arrays]
    return pl.pallas_call(
        kernel,
        out_shape=jax.ShapeDtypeStruct((ROWS, COLS), jnp.float32),
        in_specs=[pl.BlockSpec(memory_space=pl.ANY)] * 5,
        out_specs=pl.BlockSpec(memory_space=pltpu.VMEM),
        scratch_shapes=[
            pltpu.VMEM((8, 2, ROWS, COLS), jnp.bfloat16),
            pltpu.VMEM((8, 2, 2 * ROWS, COLS), jnp.bfloat16),
            pltpu.VMEM((ROWS, COLS), jnp.float32),
            pltpu.VMEM((BLOCK_ROWS, COLS), jnp.float32),
            pltpu.VMEM((2, ROWS, COLS), jnp.bfloat16),
            pltpu.VMEM((3, BLOCK_ROWS, BLOCK_COLS), jnp.int32),
            pltpu.SemaphoreType.DMA((2,)),
            pltpu.SemaphoreType.DMA((ARRIVALS,)),
            pltpu.SemaphoreType.DMA((5,)),
        ],
        compiler_params=pltpu.CompilerParams(
            collective_id=0, has_side_effects=True, vmem_limit_bytes=48 * 1024 * 1024
        ),
        name="commutator",
    )(*arrays)


def solution(mesh):
    return jax.shard_map(
        shards,
        mesh=mesh,
        in_specs=(
            P("row", "col"),
            P("row", "col"),
            P("row", "col"),
            P("row", "col"),
            P("row", "col"),
        ),
        out_specs=P("row", "col"),
        check_vma=False,
    )
```

```python
import functools

import jax
import jax.numpy as jnp
from jax import lax
from jax.experimental import pallas as pl
from jax.experimental.pallas import tpu as pltpu
from jax.sharding import PartitionSpec as P

MESH = pl.DeviceIdType.MESH
ROWS = 384
COLS = 768
BLOCK = 64
BLOCK_ROWS = ROWS // BLOCK
BLOCK_COLS = COLS // BLOCK
CUTS = (0, 128, 192, 256, 384)
CHUNKS = tuple(zip(CUTS[:-1], CUTS[1:]))
WHOLE = (0, ROWS)
ROW_EDGE = 64
COL_EDGE = 32
TAIL = 128
ARRIVALS = 39


def device_of(x, y, z, core):
    return (4 * z + 2 * (y // 2) + core, 2 * x + y % 2)


def spread(pattern):
    block_of = lax.broadcasted_iota(jnp.int32, (BLOCK_COLS, COLS), 1) // BLOCK
    index = lax.broadcasted_iota(jnp.int32, (BLOCK_COLS, COLS), 0)
    select = jnp.where(block_of == index, 1.0, 0.0).astype(jnp.float32)
    return jnp.dot(pattern.astype(jnp.float32), select, preferred_element_type=jnp.float32)


class Gather:
    def __init__(self, copy, arrival, part, place, low, ahead, behind, crossed, edge):
        self.copy, self.part, self.place, self.low = copy, part, place, low
        self.ahead, self.behind, self.crossed = ahead, behind, crossed
        self.low_edge = (ROWS - 2 * edge, ROWS - edge)
        self.high_edge = (ROWS - edge, ROWS)
        first, second, third, fourth, last = (arrival() for _ in range(5))
        self.from_behind = {(False, 0): first, (False, 1): second, (False, 2): last, (False, 3): last}
        self.from_ahead = {(False, 3): third, (False, 2): fourth, (False, 1): last, (False, 0): last}
        first, second, middle, last = (arrival() for _ in range(4))
        self.from_behind.update({(True, 3): first, (True, 1): middle, (True, 2): middle, (True, 0): last})
        self.from_ahead.update({(True, 3): second, (True, 1): middle, (True, 2): middle, (True, 0): last})
        outer, inner = arrival(), arrival()
        self.far = {0: outer, 3: outer, 1: inner, 2: inner}
        self.far_crossed, self.far_edges = arrival(), arrival()

    def k(self, offset, other):
        low = 1 - self.low if other else self.low
        return 2 * ((self.place + offset) % 4) + low

    def piece(self, offset, other, span):
        return self.part(self.k(offset, other), *span)

    def move(self, offset, other, span, target, arrival):
        piece = self.piece(offset, other, span)
        self.copy(piece, piece, target, span, arrival)

    def send_ahead(self, other, c):
        self.move(0, other, CHUNKS[c], self.ahead, self.from_behind[other, c])

    def send_behind(self, other, c):
        self.move(0, other, CHUNKS[c], self.behind, self.from_ahead[other, c])

    def pass_ahead(self, c):
        self.move(3, False, CHUNKS[c], self.ahead, self.far[c])

    def pass_behind(self, c):
        self.move(1, False, CHUNKS[c], self.behind, self.far[c])

    def pass_edges(self):
        self.from_behind[True, 3].wait()
        self.move(3, True, self.low_edge, self.ahead, self.far_edges)
        self.from_ahead[True, 3].wait()
        self.move(1, True, self.high_edge, self.behind, self.far_edges)

    def cross_far(self, c, target):
        span = (CHUNKS[c][0], min(CHUNKS[c][1], self.low_edge[0]))
        if span[0] == span[1]:
            return
        arrival = self.far_crossed if c in self.crossed else self.far_edges
        self.move(2, False, span, target, arrival)


def kernel(ham, den, h_pat, p_pat, keep, out, row, col, acc, kept, tiles, pats, send, recv, load):
    row_index = lax.axis_index("row")
    col_index = lax.axis_index("col")
    x, y_lo = col_index // 2, col_index % 2
    z, y_hi, core = row_index // 4, (row_index // 2) % 2, row_index % 2
    y = 2 * y_hi + y_lo
    right = device_of((x + 1) % 4, y, z, core)
    left = device_of((x + 3) % 4, y, z, core)
    up = device_of(x, y, (z + 1) % 4, core)
    down = device_of(x, y, (z + 3) % 4, core)
    beside = device_of(x, 2 * y_hi + 1 - y_lo, z, core)
    across = device_of(x, 2 * (1 - y_hi) + y_lo, z, core)
    opposite = device_of(x, 3 - y, z, core)
    sibling = device_of(x, y, z, 1 - core)

    barrier = pltpu.get_barrier_semaphore()
    partners = (right, left, up, down, beside, across, opposite, sibling)
    for partner in partners:
        pl.semaphore_signal(barrier, inc=1, device_id=partner, device_id_type=MESH)

    loads = []
    pairs = (
        (h_pat, pats.at[0]),
        (ham, tiles.at[0]),
        (p_pat, pats.at[1]),
        (den, tiles.at[1]),
        (keep, pats.at[2]),
    )
    for i, (source, target) in enumerate(pairs):
        made = pltpu.make_async_copy(source, target, load.at[i])
        made.start()
        loads.append(made)

    row_own = 2 * x + y_lo
    col_own = 2 * z + y_hi
    base = core * ROWS
    for matrix in range(2):
        loads[2 * matrix].wait()
        loads[2 * matrix + 1].wait()
        mask = spread(pats[matrix]).astype(jnp.bfloat16)
        for i in range(BLOCK_ROWS):
            rows = pl.ds(i * BLOCK, BLOCK)
            masked = tiles[matrix, rows, :] * mask[i : i + 1, :]
            row[row_own, matrix, rows, :] = masked
            col[col_own, matrix, pl.ds(pl.multiple_of(base + i * BLOCK, BLOCK), BLOCK), :] = masked
    loads[4].wait()
    pl.semaphore_wait(barrier, len(partners))

    def extent(count):
        if count <= 2 * ROWS:
            return col.at[0, :, pl.ds(0, count), :]
        if count <= 8 * ROWS:
            return row.at[pl.ds(0, count // ROWS)]
        return col.at[pl.ds(0, count // (2 * ROWS))]

    def described(source, landing, target, sender, arrival):
        return pltpu.make_async_remote_copy(
            src_ref=source,
            dst_ref=landing,
            send_sem=send.at[sender],
            recv_sem=recv.at[arrival],
            device_id=target,
            device_id_type=MESH,
        )

    arrivals = []

    class Arrival:
        def __init__(self):
            self.index, self.count = len(arrivals), 0
            arrivals.append(self)

        def wait(self):
            if self.count:
                area = extent(self.count)
                described(area, area, sibling, 0, self.index).wait_recv()
                self.count = 0

    sent = [0, 0]

    def copier(sender):
        def copy(source, landing, target, span, arrival):
            arrival.count += span[1] - span[0]
            sent[sender] += span[1] - span[0]
            described(source, landing, target, sender, arrival.index).start()

        return copy

    copy_row, copy_col = copier(0), copier(1)

    def row_part(k, first, last):
        return row.at[k, :, pl.ds(first, last - first), :]

    def col_part(k, first, last):
        start = pl.multiple_of(base + first, 16)
        return col.at[k, :, pl.ds(start, last - first), :]

    rows = Gather(copy_row, Arrival, row_part, x, y_lo, right, left, (0, 1, 2), ROW_EDGE)
    cols = Gather(copy_col, Arrival, col_part, z, y_hi, up, down, (0,), COL_EDGE)
    both = (rows, cols)
    crossed = [Arrival() for _ in CHUNKS]
    turned = [Arrival() for _ in CHUNKS]
    shared = [Arrival() for _ in range(5)]

    def share(stage, offset, other, span):
        cols.move(offset, other, span, sibling, shared[stage])

    def cross(c):
        rows.move(0, False, CHUNKS[c], beside, crossed[c])

    def turn(c):
        crossed[c].wait()
        landing = col_part(col_own, *CHUNKS[c])
        copy_row(rows.piece(0, True, CHUNKS[c]), landing, opposite, CHUNKS[c], turned[c])

    def kind_of(place, low, k):
        distance = (k // 2 - place + 4) % 4
        other = (k % 2 + low) % 2
        late = jnp.where(distance == 2, 2, 1)
        return jnp.where((other == 0) | (distance == 0), 0, late)

    def product(k, out_part, inner_part):
        out_span = slice(*out_part)
        if inner_part == WHOLE:
            inner_spans = [slice(None)]
        else:
            inner_spans = [slice(base + inner_part[0], base + inner_part[1]) for base in (0, ROWS)]

        def left(matrix):
            pieces = [row[k, matrix, out_span, inner] for inner in inner_spans]
            return jnp.concatenate(pieces, axis=1)

        def right(matrix):
            return jnp.concatenate([col[k, matrix, inner, :] for inner in inner_spans], axis=0)

        forward = jnp.dot(left(0), right(1), preferred_element_type=jnp.float32)
        backward = jnp.dot(left(1), right(0), preferred_element_type=jnp.float32)
        acc[out_span, :] += forward - backward

    def visit(k, r, c, entries):
        for row_kinds, col_kinds, *parts in entries:
            fits = [(r == kind) & (c == other) for kind in row_kinds for other in col_kinds]

            @pl.when(functools.reduce(jnp.logical_or, fits))
            def _():
                for out_part, inner_part in parts:
                    product(k, out_part, inner_part)

    def stage(*entries):
        @pl.loop(0, 8)
        def _(k):
            visit(k, kind_of(x, y_lo, k), kind_of(z, y_hi, k), entries)

    def stage_of(g, kind, *entries):
        def body(offset):
            k = g.k(offset, True)
            if g is rows:
                visit(k, kind, kind_of(z, y_hi, k), entries)
            else:
                visit(k, kind_of(x, y_lo, k), kind, entries)

        if kind == 2:
            body(2)
        else:

            @pl.loop(0, 2)
            def _(i):
                body(1 + 2 * i)

    near_first, near_last = (TAIL, ROWS), (0, TAIL)
    far_rows_first, far_rows_last = (0, 2 * TAIL), (2 * TAIL, ROWS)
    far_cols_first, far_cols_last = (0, TAIL), (TAIL, ROWS)

    for first, second in ((0, 3), (1, 2)):
        for g in both:
            g.send_ahead(False, first)
            g.send_behind(False, second)
        if first == 0:
            cross(3)
            cross(1)
    cross(2)
    cross(0)
    share(0, 0, False, WHOLE)
    acc[...] = jnp.zeros_like(acc)
    kept[...] = spread(pats[2])

    for first, second in ((0, 3), (1, 2)):
        for g in both:
            g.from_behind[False, first].wait()
            g.pass_ahead(first)
            g.from_ahead[False, second].wait()
            g.pass_behind(second)
        if first == 0:
            turn(3)
    for first, second in ((2, 1), (3, 0)):
        for g in both:
            g.send_ahead(False, first)
            g.send_behind(False, second)
    turn(1)
    turn(2)

    def cross_far(g, target, *chunks):
        for c in chunks:
            g.far[c].wait()
            g.cross_far(c, target)

    cross_far(rows, beside, 0)
    turn(0)
    for c in (3, 1, 2):
        rows.send_ahead(True, c)
        rows.send_behind(True, c)
    cross_far(rows, beside, 1, 2, 3)
    for c in (3, 1, 2, 0):
        turned[c].wait()
        cols.send_ahead(True, c)
        cols.send_behind(True, c)
    share(0, 0, True, WHOLE)
    cross_far(cols, across, 0, 1, 2, 3)
    share(0, 2, False, WHOLE)
    for g in both:
        g.from_behind[False, 3].wait()
    share(0, 3, False, WHOLE)
    share(0, 1, False, WHOLE)
    rows.pass_edges()
    rows.send_ahead(True, 0)
    rows.send_behind(True, 0)
    cols.pass_edges()
    shared[0].wait()
    stage(((0,), (0,), (WHOLE, WHOLE)))

    rows.far_crossed.wait()
    stage_of(rows, 2, ((2,), (0,), (far_rows_first, WHOLE)))

    cols.from_behind[True, 1].wait()
    share(1, 3, True, near_first)
    share(1, 1, True, near_first)
    cols.far_crossed.wait()
    share(2, 2, True, far_cols_first)
    rows.from_behind[True, 1].wait()
    shared[1].wait()
    shared[2].wait()
    stage(
        ((1,), (0,), (near_first, WHOLE)),
        ((0,), (1,), (WHOLE, near_first)),
        ((1,), (1,), (near_first, near_first)),
        ((2,), (1,), (far_rows_first, near_first)),
        ((0,), (2,), (WHOLE, far_cols_first)),
        ((1,), (2,), (near_first, far_cols_first)),
        ((2,), (2,), (far_rows_first, far_cols_first)),
    )

    rows.far_edges.wait()
    stage_of(
        rows,
        2,
        ((2,), (0,), (far_rows_last, WHOLE)),
        ((2,), (1,), (far_rows_last, near_first)),
        ((2,), (2,), (far_rows_last, far_cols_first)),
    )

    cols.from_behind[True, 0].wait()
    share(3, 3, True, near_last)
    share(3, 1, True, near_last)
    shared[3].wait()
    stage_of(
        cols,
        1,
        ((0, 2), (1,), (WHOLE, near_last)),
        ((1,), (1,), (near_first, near_last)),
    )

    cols.far_edges.wait()
    share(4, 2, True, far_cols_last)
    rows.from_behind[True, 0].wait()
    stage_of(
        rows,
        1,
        ((1,), (0, 1), (near_last, WHOLE)),
        ((1,), (2,), (near_last, far_cols_first)),
    )
    shared[4].wait()
    product(cols.k(2, True), WHOLE, far_cols_last)

    for i in range(BLOCK_ROWS):
        block_rows = pl.ds(i * BLOCK, BLOCK)
        out[block_rows, :] = acc[block_rows, :] * kept[i : i + 1, :]
    for sender, count in enumerate(sent):
        area = extent(count)
        described(area, area, sibling, sender, 0).wait_send()


def shards(*arrays):
    arrays = [pltpu.with_memory_space_constraint(array, pltpu.HBM) for array in arrays]
    return pl.pallas_call(
        kernel,
        out_shape=jax.ShapeDtypeStruct((ROWS, COLS), jnp.float32),
        in_specs=[pl.BlockSpec(memory_space=pl.ANY)] * 5,
        out_specs=pl.BlockSpec(memory_space=pltpu.VMEM),
        scratch_shapes=[
            pltpu.VMEM((8, 2, ROWS, COLS), jnp.bfloat16),
            pltpu.VMEM((8, 2, 2 * ROWS, COLS), jnp.bfloat16),
            pltpu.VMEM((ROWS, COLS), jnp.float32),
            pltpu.VMEM((BLOCK_ROWS, COLS), jnp.float32),
            pltpu.VMEM((2, ROWS, COLS), jnp.bfloat16),
            pltpu.VMEM((3, BLOCK_ROWS, BLOCK_COLS), jnp.int32),
            pltpu.SemaphoreType.DMA((2,)),
            pltpu.SemaphoreType.DMA((ARRIVALS,)),
            pltpu.SemaphoreType.DMA((5,)),
        ],
        compiler_params=pltpu.CompilerParams(
            collective_id=0, has_side_effects=True, vmem_limit_bytes=48 * 1024 * 1024
        ),
        name="commutator",
    )(*arrays)


def solution(mesh):
    return jax.shard_map(
        shards,
        mesh=mesh,
        in_specs=(
            P("row", "col"),
            P("row", "col"),
            P("row", "col"),
            P("row", "col"),
            P("row", "col"),
        ),
        out_specs=P("row", "col"),
        check_vma=False,
    )
```

```python
import functools

import jax
import jax.numpy as jnp
from jax import lax
from jax.experimental import pallas as pl
from jax.experimental.pallas import tpu as pltpu
from jax.sharding import PartitionSpec as P

MESH = pl.DeviceIdType.MESH
ROWS = 384
COLS = 768
BLOCK = 64
BLOCK_ROWS = ROWS // BLOCK
BLOCK_COLS = COLS // BLOCK
CUTS = (0, 128, 192, 256, 384)
CHUNKS = tuple(zip(CUTS[:-1], CUTS[1:]))
WHOLE = (0, ROWS)
ROW_EDGE = 64
COL_EDGE = 32
TAIL = 128
ARRIVALS = 39


def device_of(x, y, z, core):
    return (4 * z + 2 * (y // 2) + core, 2 * x + y % 2)


def spread(pattern):
    block_of = lax.broadcasted_iota(jnp.int32, (BLOCK_COLS, COLS), 1) // BLOCK
    index = lax.broadcasted_iota(jnp.int32, (BLOCK_COLS, COLS), 0)
    select = jnp.where(block_of == index, 1.0, 0.0).astype(jnp.float32)
    return jnp.dot(pattern.astype(jnp.float32), select, preferred_element_type=jnp.float32)


class Gather:
    def __init__(self, copy, arrival, part, place, low, ahead, behind, edge):
        self.copy, self.part, self.place, self.low = copy, part, place, low
        self.ahead, self.behind = ahead, behind
        self.low_edge = (ROWS - 2 * edge, ROWS - edge)
        self.high_edge = (ROWS - edge, ROWS)
        first, second, third, fourth, last = (arrival() for _ in range(5))
        self.from_behind = {(False, 0): first, (False, 1): second, (False, 2): last, (False, 3): last}
        self.from_ahead = {(False, 3): third, (False, 2): fourth, (False, 1): last, (False, 0): last}
        first, second, middle, last = (arrival() for _ in range(4))
        self.from_behind.update({(True, 3): first, (True, 1): middle, (True, 2): middle, (True, 0): last})
        self.from_ahead.update({(True, 3): second, (True, 1): middle, (True, 2): middle, (True, 0): last})
        outer, inner = arrival(), arrival()
        self.far = {0: outer, 3: outer, 1: inner, 2: inner}
        self.far_crossed, self.far_edges = arrival(), arrival()

    def k(self, offset, other):
        low = 1 - self.low if other else self.low
        return 2 * ((self.place + offset) % 4) + low

    def piece(self, offset, other, span):
        return self.part(self.k(offset, other), *span)

    def move(self, offset, other, span, target, arrival):
        piece = self.piece(offset, other, span)
        self.copy(piece, piece, target, span, arrival)

    def send_ahead(self, other, c):
        self.move(0, other, CHUNKS[c], self.ahead, self.from_behind[other, c])

    def send_behind(self, other, c):
        self.move(0, other, CHUNKS[c], self.behind, self.from_ahead[other, c])

    def send_second_half(self):
        self.move(0, False, (CUTS[2], ROWS), self.ahead, self.from_behind[False, 3])
        self.move(0, False, (0, CUTS[2]), self.behind, self.from_ahead[False, 0])

    def send_middle(self):
        span = (CUTS[1], CUTS[3])
        self.move(0, True, span, self.ahead, self.from_behind[True, 1])
        self.move(0, True, span, self.behind, self.from_ahead[True, 1])

    def pass_ahead(self, c):
        self.move(3, False, CHUNKS[c], self.ahead, self.far[c])

    def pass_behind(self, c):
        self.move(1, False, CHUNKS[c], self.behind, self.far[c])

    def pass_edges(self):
        self.from_behind[True, 3].wait()
        self.move(3, True, self.low_edge, self.ahead, self.far_edges)
        self.from_ahead[True, 3].wait()
        self.move(1, True, self.high_edge, self.behind, self.far_edges)

    def cross_far_first(self, target):
        self.far[0].wait()
        self.move(2, False, CHUNKS[0], target, self.far_crossed)

    def cross_far_rest(self, target, arrival):
        self.far[1].wait()
        self.move(2, False, (CUTS[1], self.low_edge[0]), target, arrival)


def kernel(ham, den, h_pat, p_pat, keep, out, row, col, acc, kept, tiles, pats, send, recv, load):
    row_index = lax.axis_index("row")
    col_index = lax.axis_index("col")
    x, y_lo = col_index // 2, col_index % 2
    z, y_hi, core = row_index // 4, (row_index // 2) % 2, row_index % 2
    y = 2 * y_hi + y_lo
    right = device_of((x + 1) % 4, y, z, core)
    left = device_of((x + 3) % 4, y, z, core)
    up = device_of(x, y, (z + 1) % 4, core)
    down = device_of(x, y, (z + 3) % 4, core)
    beside = device_of(x, 2 * y_hi + 1 - y_lo, z, core)
    across = device_of(x, 2 * (1 - y_hi) + y_lo, z, core)
    opposite = device_of(x, 3 - y, z, core)
    sibling = device_of(x, y, z, 1 - core)

    barrier = pltpu.get_barrier_semaphore()
    partners = (right, left, up, down, beside, across, opposite, sibling)
    for partner in partners:
        pl.semaphore_signal(barrier, inc=1, device_id=partner, device_id_type=MESH)

    loads = []
    pairs = (
        (h_pat, pats.at[0]),
        (ham, tiles.at[0]),
        (p_pat, pats.at[1]),
        (den, tiles.at[1]),
        (keep, pats.at[2]),
    )
    for i, (source, target) in enumerate(pairs):
        made = pltpu.make_async_copy(source, target, load.at[i])
        made.start()
        loads.append(made)

    row_own = 2 * x + y_lo
    col_own = 2 * z + y_hi
    base = core * ROWS
    for matrix in range(2):
        loads[2 * matrix].wait()
        loads[2 * matrix + 1].wait()
        mask = spread(pats[matrix]).astype(jnp.bfloat16)
        for i in range(BLOCK_ROWS):
            rows = pl.ds(i * BLOCK, BLOCK)
            masked = tiles[matrix, rows, :] * mask[i : i + 1, :]
            row[row_own, matrix, rows, :] = masked
            col[col_own, matrix, pl.ds(pl.multiple_of(base + i * BLOCK, BLOCK), BLOCK), :] = masked
    loads[4].wait()
    pl.semaphore_wait(barrier, len(partners))

    def extent(count):
        if count <= 2 * ROWS:
            return col.at[0, :, pl.ds(0, count), :]
        if count <= 8 * ROWS:
            return row.at[pl.ds(0, count // ROWS)]
        return col.at[pl.ds(0, count // (2 * ROWS))]

    def described(source, landing, target, sender, arrival):
        return pltpu.make_async_remote_copy(
            src_ref=source,
            dst_ref=landing,
            send_sem=send.at[sender],
            recv_sem=recv.at[arrival],
            device_id=target,
            device_id_type=MESH,
        )

    arrivals = []

    class Arrival:
        def __init__(self):
            self.index, self.count = len(arrivals), 0
            arrivals.append(self)

        def wait(self):
            if self.count:
                area = extent(self.count)
                described(area, area, sibling, 0, self.index).wait_recv()
                self.count = 0

    sent = [0, 0]

    def copier(sender):
        def copy(source, landing, target, span, arrival):
            arrival.count += span[1] - span[0]
            sent[sender] += span[1] - span[0]
            described(source, landing, target, sender, arrival.index).start()

        return copy

    copy_row, copy_col = copier(0), copier(1)

    def row_part(k, first, last):
        return row.at[k, :, pl.ds(first, last - first), :]

    def col_part(k, first, last):
        start = pl.multiple_of(base + first, 16)
        return col.at[k, :, pl.ds(start, last - first), :]

    rows = Gather(copy_row, Arrival, row_part, x, y_lo, right, left, ROW_EDGE)
    cols = Gather(copy_col, Arrival, col_part, z, y_hi, up, down, COL_EDGE)
    both = (rows, cols)
    crossed = [Arrival() for _ in CHUNKS]
    turned = [Arrival() for _ in CHUNKS]
    shared = [Arrival() for _ in range(5)]

    def share(stage, offset, other, span):
        cols.move(offset, other, span, sibling, shared[stage])

    def cross(c):
        rows.move(0, False, CHUNKS[c], beside, crossed[c])

    def turn(c):
        crossed[c].wait()
        landing = col_part(col_own, *CHUNKS[c])
        copy_row(rows.piece(0, True, CHUNKS[c]), landing, opposite, CHUNKS[c], turned[c])

    def kind_of(place, low, k):
        distance = (k // 2 - place + 4) % 4
        other = (k % 2 + low) % 2
        late = jnp.where(distance == 2, 2, 1)
        return jnp.where((other == 0) | (distance == 0), 0, late)

    def product(k, out_part, inner_part):
        out_span = slice(*out_part)
        if inner_part == WHOLE:
            inner_spans = [slice(None)]
        else:
            inner_spans = [slice(base + inner_part[0], base + inner_part[1]) for base in (0, ROWS)]

        def left(matrix):
            pieces = [row[k, matrix, out_span, inner] for inner in inner_spans]
            return jnp.concatenate(pieces, axis=1)

        def right(matrix):
            return jnp.concatenate([col[k, matrix, inner, :] for inner in inner_spans], axis=0)

        forward = jnp.dot(left(0), right(1), preferred_element_type=jnp.float32)
        backward = jnp.dot(left(1), right(0), preferred_element_type=jnp.float32)
        acc[out_span, :] += forward - backward

    def visit(k, r, c, entries):
        for row_kinds, col_kinds, *parts in entries:
            fits = [(r == kind) & (c == other) for kind in row_kinds for other in col_kinds]

            @pl.when(functools.reduce(jnp.logical_or, fits))
            def _():
                for out_part, inner_part in parts:
                    product(k, out_part, inner_part)

    def stage(*entries):
        @pl.loop(0, 8)
        def _(k):
            visit(k, kind_of(x, y_lo, k), kind_of(z, y_hi, k), entries)

    def stage_of(g, kind, *entries):
        def body(offset):
            k = g.k(offset, True)
            if g is rows:
                visit(k, kind, kind_of(z, y_hi, k), entries)
            else:
                visit(k, kind_of(x, y_lo, k), kind, entries)

        if kind == 2:
            body(2)
        else:

            @pl.loop(0, 2)
            def _(i):
                body(1 + 2 * i)

    near_first, near_last = (TAIL, ROWS), (0, TAIL)
    far_rows_first, far_rows_last = (0, 2 * TAIL), (2 * TAIL, ROWS)
    far_cols_first, far_cols_last = (0, TAIL), (TAIL, ROWS)

    for first, second in ((0, 3), (1, 2)):
        for g in both:
            g.send_ahead(False, first)
            g.send_behind(False, second)
        if first == 0:
            cross(3)
            cross(1)
    cross(2)
    cross(0)
    share(0, 0, False, WHOLE)
    acc[...] = jnp.zeros_like(acc)
    kept[...] = spread(pats[2])

    for first, second in ((0, 3), (1, 2)):
        for g in both:
            g.from_behind[False, first].wait()
            g.pass_ahead(first)
            g.from_ahead[False, second].wait()
            g.pass_behind(second)
        if first == 0:
            turn(3)
    for g in both:
        g.send_second_half()
    turn(1)
    turn(2)

    rows.cross_far_first(beside)
    turn(0)
    rows.send_ahead(True, 3)
    rows.send_behind(True, 3)
    rows.send_middle()
    rows.cross_far_rest(beside, rows.far_crossed)
    cols.cross_far_first(across)
    cols.cross_far_rest(across, cols.far_edges)
    share(0, 2, False, WHOLE)
    turned[3].wait()
    cols.send_ahead(True, 3)
    cols.send_behind(True, 3)
    turned[1].wait()
    turned[2].wait()
    cols.send_middle()
    turned[0].wait()
    cols.send_ahead(True, 0)
    cols.send_behind(True, 0)
    share(0, 0, True, WHOLE)
    for g in both:
        g.from_behind[False, 3].wait()
    share(0, 3, False, WHOLE)
    share(0, 1, False, WHOLE)
    rows.pass_edges()
    rows.send_ahead(True, 0)
    rows.send_behind(True, 0)
    cols.pass_edges()
    shared[0].wait()
    stage(((0,), (0,), (WHOLE, WHOLE)))

    rows.far_crossed.wait()
    stage_of(rows, 2, ((2,), (0,), (far_rows_first, WHOLE)))

    cols.from_behind[True, 1].wait()
    share(1, 3, True, near_first)
    share(1, 1, True, near_first)
    cols.far_crossed.wait()
    share(2, 2, True, far_cols_first)
    rows.from_behind[True, 1].wait()
    shared[1].wait()
    shared[2].wait()
    stage(
        ((1,), (0,), (near_first, WHOLE)),
        ((0,), (1,), (WHOLE, near_first)),
        ((1,), (1,), (near_first, near_first)),
        ((2,), (1,), (far_rows_first, near_first)),
        ((0,), (2,), (WHOLE, far_cols_first)),
        ((1,), (2,), (near_first, far_cols_first)),
        ((2,), (2,), (far_rows_first, far_cols_first)),
    )

    rows.far_edges.wait()
    stage_of(
        rows,
        2,
        ((2,), (0,), (far_rows_last, WHOLE)),
        ((2,), (1,), (far_rows_last, near_first)),
        ((2,), (2,), (far_rows_last, far_cols_first)),
    )

    cols.from_behind[True, 0].wait()
    share(3, 3, True, near_last)
    share(3, 1, True, near_last)
    shared[3].wait()
    stage_of(
        cols,
        1,
        ((0, 2), (1,), (WHOLE, near_last)),
        ((1,), (1,), (near_first, near_last)),
    )

    cols.far_edges.wait()
    share(4, 2, True, far_cols_last)
    rows.from_behind[True, 0].wait()
    stage_of(
        rows,
        1,
        ((1,), (0, 1), (near_last, WHOLE)),
        ((1,), (2,), (near_last, far_cols_first)),
    )
    shared[4].wait()
    product(cols.k(2, True), WHOLE, far_cols_last)

    for i in range(BLOCK_ROWS):
        block_rows = pl.ds(i * BLOCK, BLOCK)
        out[block_rows, :] = acc[block_rows, :] * kept[i : i + 1, :]
    for sender, count in enumerate(sent):
        area = extent(count)
        described(area, area, sibling, sender, 0).wait_send()


def shards(*arrays):
    arrays = [pltpu.with_memory_space_constraint(array, pltpu.HBM) for array in arrays]
    return pl.pallas_call(
        kernel,
        out_shape=jax.ShapeDtypeStruct((ROWS, COLS), jnp.float32),
        in_specs=[pl.BlockSpec(memory_space=pl.ANY)] * 5,
        out_specs=pl.BlockSpec(memory_space=pltpu.VMEM),
        scratch_shapes=[
            pltpu.VMEM((8, 2, ROWS, COLS), jnp.bfloat16),
            pltpu.VMEM((8, 2, 2 * ROWS, COLS), jnp.bfloat16),
            pltpu.VMEM((ROWS, COLS), jnp.float32),
            pltpu.VMEM((BLOCK_ROWS, COLS), jnp.float32),
            pltpu.VMEM((2, ROWS, COLS), jnp.bfloat16),
            pltpu.VMEM((3, BLOCK_ROWS, BLOCK_COLS), jnp.int32),
            pltpu.SemaphoreType.DMA((2,)),
            pltpu.SemaphoreType.DMA((ARRIVALS,)),
            pltpu.SemaphoreType.DMA((5,)),
        ],
        compiler_params=pltpu.CompilerParams(
            collective_id=0, has_side_effects=True, vmem_limit_bytes=48 * 1024 * 1024
        ),
        name="commutator",
    )(*arrays)


def solution(mesh):
    return jax.shard_map(
        shards,
        mesh=mesh,
        in_specs=(
            P("row", "col"),
            P("row", "col"),
            P("row", "col"),
            P("row", "col"),
            P("row", "col"),
        ),
        out_specs=P("row", "col"),
        check_vma=False,
    )
```

```python
import functools

import jax
import jax.numpy as jnp
from jax import lax
from jax.experimental import pallas as pl
from jax.experimental.pallas import tpu as pltpu
from jax.sharding import PartitionSpec as P

MESH = pl.DeviceIdType.MESH
ROWS = 384
COLS = 768
BLOCK = 64
BLOCK_ROWS = ROWS // BLOCK
BLOCK_COLS = COLS // BLOCK
CUTS = (0, 128, 192, 256, 384)
CHUNKS = tuple(zip(CUTS[:-1], CUTS[1:]))
WHOLE = (0, ROWS)
ROW_EDGE = 64
COL_EDGE = 32
TAIL = 128
ARRIVALS = 40


def device_of(x, y, z, core):
    return (4 * z + 2 * (y // 2) + core, 2 * x + y % 2)


def spread(pattern):
    block_of = lax.broadcasted_iota(jnp.int32, (BLOCK_COLS, COLS), 1) // BLOCK
    index = lax.broadcasted_iota(jnp.int32, (BLOCK_COLS, COLS), 0)
    select = jnp.where(block_of == index, 1.0, 0.0).astype(jnp.float32)
    return jnp.dot(pattern.astype(jnp.float32), select, preferred_element_type=jnp.float32)


class Gather:
    def __init__(self, copy, arrival, part, place, low, ahead, behind, crossed, edge):
        self.copy, self.part, self.place, self.low = copy, part, place, low
        self.ahead, self.behind, self.crossed = ahead, behind, crossed
        self.low_edge = (ROWS - 2 * edge, ROWS - edge)
        self.high_edge = (ROWS - edge, ROWS)
        first, second, third, fourth, last = (arrival() for _ in range(5))
        self.from_behind = {(False, 0): first, (False, 1): second, (False, 2): last, (False, 3): last}
        self.from_ahead = {(False, 3): third, (False, 2): fourth, (False, 1): last, (False, 0): last}
        first, second, middle, last = (arrival() for _ in range(4))
        self.from_behind.update({(True, 3): first, (True, 1): middle, (True, 2): middle, (True, 0): last})
        self.from_ahead.update({(True, 3): second, (True, 1): middle, (True, 2): middle, (True, 0): last})
        outer, inner = arrival(), arrival()
        self.far = {0: outer, 3: outer, 1: inner, 2: inner}
        self.far_crossed, self.far_edges = arrival(), arrival()

    def k(self, offset, other):
        low = 1 - self.low if other else self.low
        return 2 * ((self.place + offset) % 4) + low

    def piece(self, offset, other, span):
        return self.part(self.k(offset, other), *span)

    def move(self, offset, other, span, target, arrival):
        piece = self.piece(offset, other, span)
        self.copy(piece, piece, target, span, arrival)

    def send_ahead(self, other, c):
        self.move(0, other, CHUNKS[c], self.ahead, self.from_behind[other, c])

    def send_behind(self, other, c):
        self.move(0, other, CHUNKS[c], self.behind, self.from_ahead[other, c])

    def pass_ahead(self, c):
        self.move(3, False, CHUNKS[c], self.ahead, self.far[c])

    def pass_behind(self, c):
        self.move(1, False, CHUNKS[c], self.behind, self.far[c])

    def pass_edges(self):
        self.from_behind[True, 3].wait()
        self.move(3, True, self.low_edge, self.ahead, self.far_edges)
        self.from_ahead[True, 3].wait()
        self.move(1, True, self.high_edge, self.behind, self.far_edges)

    def cross_far(self, c, target):
        span = (CHUNKS[c][0], min(CHUNKS[c][1], self.low_edge[0]))
        if span[0] == span[1]:
            return
        arrival = self.far_crossed if c in self.crossed else self.far_edges
        self.move(2, False, span, target, arrival)


def kernel(ham, den, h_pat, p_pat, keep, out, row, col, acc, kept, tiles, pats, send, recv, load):
    row_index = lax.axis_index("row")
    col_index = lax.axis_index("col")
    x, y_lo = col_index // 2, col_index % 2
    z, y_hi, core = row_index // 4, (row_index // 2) % 2, row_index % 2
    y = 2 * y_hi + y_lo
    right = device_of((x + 1) % 4, y, z, core)
    left = device_of((x + 3) % 4, y, z, core)
    up = device_of(x, y, (z + 1) % 4, core)
    down = device_of(x, y, (z + 3) % 4, core)
    beside = device_of(x, 2 * y_hi + 1 - y_lo, z, core)
    across = device_of(x, 2 * (1 - y_hi) + y_lo, z, core)
    opposite = device_of(x, 3 - y, z, core)
    sibling = device_of(x, y, z, 1 - core)

    barrier = pltpu.get_barrier_semaphore()
    partners = (right, left, up, down, beside, across, opposite, sibling)
    for partner in partners:
        pl.semaphore_signal(barrier, inc=1, device_id=partner, device_id_type=MESH)

    loads = []
    pairs = (
        (h_pat, pats.at[0]),
        (ham, tiles.at[0]),
        (p_pat, pats.at[1]),
        (den, tiles.at[1]),
        (keep, pats.at[2]),
    )
    for i, (source, target) in enumerate(pairs):
        made = pltpu.make_async_copy(source, target, load.at[i])
        made.start()
        loads.append(made)

    row_own = 2 * x + y_lo
    col_own = 2 * z + y_hi
    base = core * ROWS
    for matrix in range(2):
        loads[2 * matrix].wait()
        loads[2 * matrix + 1].wait()
        mask = spread(pats[matrix]).astype(jnp.bfloat16)
        for i in range(BLOCK_ROWS):
            rows = pl.ds(i * BLOCK, BLOCK)
            masked = tiles[matrix, rows, :] * mask[i : i + 1, :]
            row[row_own, matrix, rows, :] = masked
            col[col_own, matrix, pl.ds(pl.multiple_of(base + i * BLOCK, BLOCK), BLOCK), :] = masked
    loads[4].wait()
    pl.semaphore_wait(barrier, len(partners))

    def extent(count):
        if count <= 2 * ROWS:
            return col.at[0, :, pl.ds(0, count), :]
        if count <= 8 * ROWS:
            return row.at[pl.ds(0, count // ROWS)]
        return col.at[pl.ds(0, count // (2 * ROWS))]

    def described(source, landing, target, sender, arrival):
        return pltpu.make_async_remote_copy(
            src_ref=source,
            dst_ref=landing,
            send_sem=send.at[sender],
            recv_sem=recv.at[arrival],
            device_id=target,
            device_id_type=MESH,
        )

    arrivals = []

    class Arrival:
        def __init__(self):
            self.index, self.count = len(arrivals), 0
            arrivals.append(self)

        def wait(self):
            if self.count:
                area = extent(self.count)
                described(area, area, sibling, 0, self.index).wait_recv()
                self.count = 0

    sent = [0, 0]

    def copier(sender):
        def copy(source, landing, target, span, arrival):
            arrival.count += span[1] - span[0]
            sent[sender] += span[1] - span[0]
            described(source, landing, target, sender, arrival.index).start()

        return copy

    copy_row, copy_col = copier(0), copier(1)

    def row_part(k, first, last):
        return row.at[k, :, pl.ds(first, last - first), :]

    def col_part(k, first, last):
        start = pl.multiple_of(base + first, 16)
        return col.at[k, :, pl.ds(start, last - first), :]

    rows = Gather(copy_row, Arrival, row_part, x, y_lo, right, left, (0, 1, 2), ROW_EDGE)
    cols = Gather(copy_col, Arrival, col_part, z, y_hi, up, down, (0,), COL_EDGE)
    both = (rows, cols)
    crossed = [Arrival() for _ in CHUNKS]
    turned = [Arrival() for _ in CHUNKS]
    shared = [Arrival() for _ in range(6)]

    def share(stage, offset, other, span):
        cols.move(offset, other, span, sibling, shared[stage])

    def cross(c):
        rows.move(0, False, CHUNKS[c], beside, crossed[c])

    def turn(c):
        crossed[c].wait()
        landing = col_part(col_own, *CHUNKS[c])
        copy_row(rows.piece(0, True, CHUNKS[c]), landing, opposite, CHUNKS[c], turned[c])

    def kind_of(place, low, k):
        distance = (k // 2 - place + 4) % 4
        other = (k % 2 + low) % 2
        late = jnp.where(distance == 2, 2, 1)
        return jnp.where((other == 0) | (distance == 0), 0, late)

    def product(k, out_part, inner_part):
        out_span = slice(*out_part)
        if inner_part == WHOLE:
            inner_spans = [slice(None)]
        else:
            inner_spans = [slice(base + inner_part[0], base + inner_part[1]) for base in (0, ROWS)]

        def left(matrix):
            pieces = [row[k, matrix, out_span, inner] for inner in inner_spans]
            return jnp.concatenate(pieces, axis=1)

        def right(matrix):
            return jnp.concatenate([col[k, matrix, inner, :] for inner in inner_spans], axis=0)

        forward = jnp.dot(left(0), right(1), preferred_element_type=jnp.float32)
        backward = jnp.dot(left(1), right(0), preferred_element_type=jnp.float32)
        acc[out_span, :] += forward - backward

    def visit(k, r, c, entries):
        for row_kinds, col_kinds, *parts in entries:
            fits = [(r == kind) & (c == other) for kind in row_kinds for other in col_kinds]

            @pl.when(functools.reduce(jnp.logical_or, fits))
            def _():
                for out_part, inner_part in parts:
                    product(k, out_part, inner_part)

    def stage(*entries):
        @pl.loop(0, 8)
        def _(k):
            visit(k, kind_of(x, y_lo, k), kind_of(z, y_hi, k), entries)

    def stage_of(g, kind, *entries):
        def body(offset):
            k = g.k(offset, True)
            if g is rows:
                visit(k, kind, kind_of(z, y_hi, k), entries)
            else:
                visit(k, kind_of(x, y_lo, k), kind, entries)

        if kind == 2:
            body(2)
        else:

            @pl.loop(0, 2)
            def _(i):
                body(1 + 2 * i)

    near_first, near_last = (TAIL, ROWS), (0, TAIL)
    far_rows_first, far_rows_last = (0, 2 * TAIL), (2 * TAIL, ROWS)
    far_cols_first, far_cols_last = (0, TAIL), (TAIL, ROWS)

    for first, second in ((0, 3), (1, 2)):
        for g in both:
            g.send_ahead(False, first)
            g.send_behind(False, second)
        if first == 0:
            cross(3)
            cross(1)
    cross(2)
    cross(0)
    share(0, 0, False, WHOLE)
    acc[...] = jnp.zeros_like(acc)
    kept[...] = spread(pats[2])

    for first, second in ((0, 3), (1, 2)):
        for g in both:
            g.from_behind[False, first].wait()
            g.pass_ahead(first)
            g.from_ahead[False, second].wait()
            g.pass_behind(second)
        if first == 0:
            turn(3)
    for first, second in ((2, 1), (3, 0)):
        for g in both:
            g.send_ahead(False, first)
            g.send_behind(False, second)
    turn(1)
    turn(2)

    def cross_far(g, target, *chunks):
        for c in chunks:
            g.far[c].wait()
            g.cross_far(c, target)

    cross_far(rows, beside, 0)
    turn(0)
    for c in (3, 1, 2):
        rows.send_ahead(True, c)
        rows.send_behind(True, c)
    cross_far(rows, beside, 1, 2, 3)
    for c in (3, 1, 2, 0):
        turned[c].wait()
        cols.send_ahead(True, c)
        cols.send_behind(True, c)
    share(0, 0, True, WHOLE)
    cross_far(cols, across, 0, 1, 2, 3)
    share(0, 2, False, WHOLE)
    for g in both:
        g.from_behind[False, 3].wait()
    share(0, 3, False, WHOLE)
    share(0, 1, False, WHOLE)
    rows.pass_edges()
    rows.send_ahead(True, 0)
    rows.send_behind(True, 0)
    cols.pass_edges()
    shared[0].wait()
    stage(((0,), (0,), (WHOLE, WHOLE)))

    rows.far_crossed.wait()
    stage_of(rows, 2, ((2,), (0,), (far_rows_first, WHOLE)))

    cols.from_behind[True, 1].wait()
    share(1, 3, True, near_first)
    share(1, 1, True, near_first)
    cols.far_crossed.wait()
    share(2, 2, True, far_cols_first)
    rows.from_behind[True, 1].wait()
    shared[1].wait()
    shared[2].wait()
    stage(
        ((1,), (0,), (near_first, WHOLE)),
        ((0,), (1,), (WHOLE, near_first)),
        ((1,), (1,), (near_first, near_first)),
        ((2,), (1,), (far_rows_first, near_first)),
        ((0,), (2,), (WHOLE, far_cols_first)),
        ((1,), (2,), (near_first, far_cols_first)),
        ((2,), (2,), (far_rows_first, far_cols_first)),
    )

    rows.far_edges.wait()
    stage_of(
        rows,
        2,
        ((2,), (0,), (far_rows_last, WHOLE)),
        ((2,), (1,), (far_rows_last, near_first)),
        ((2,), (2,), (far_rows_last, far_cols_first)),
    )

    cols.from_behind[True, 0].wait()
    share(3, 1, True, near_last)
    share(5, 3, True, near_last)
    for arrived, offset in ((3, 1), (5, 3)):
        shared[arrived].wait()
        k = cols.k(offset, True)
        visit(
            k,
            kind_of(x, y_lo, k),
            1,
            (
                ((0, 2), (1,), (WHOLE, near_last)),
                ((1,), (1,), (near_first, near_last)),
            ),
        )

    cols.far_edges.wait()
    share(4, 2, True, far_cols_last)
    rows.from_behind[True, 0].wait()
    stage_of(
        rows,
        1,
        ((1,), (0, 1), (near_last, WHOLE)),
        ((1,), (2,), (near_last, far_cols_first)),
    )
    shared[4].wait()
    product(cols.k(2, True), WHOLE, far_cols_last)

    for i in range(BLOCK_ROWS):
        block_rows = pl.ds(i * BLOCK, BLOCK)
        out[block_rows, :] = acc[block_rows, :] * kept[i : i + 1, :]
    for sender, count in enumerate(sent):
        area = extent(count)
        described(area, area, sibling, sender, 0).wait_send()


def shards(*arrays):
    arrays = [pltpu.with_memory_space_constraint(array, pltpu.HBM) for array in arrays]
    return pl.pallas_call(
        kernel,
        out_shape=jax.ShapeDtypeStruct((ROWS, COLS), jnp.float32),
        in_specs=[pl.BlockSpec(memory_space=pl.ANY)] * 5,
        out_specs=pl.BlockSpec(memory_space=pltpu.VMEM),
        scratch_shapes=[
            pltpu.VMEM((8, 2, ROWS, COLS), jnp.bfloat16),
            pltpu.VMEM((8, 2, 2 * ROWS, COLS), jnp.bfloat16),
            pltpu.VMEM((ROWS, COLS), jnp.float32),
            pltpu.VMEM((BLOCK_ROWS, COLS), jnp.float32),
            pltpu.VMEM((2, ROWS, COLS), jnp.bfloat16),
            pltpu.VMEM((3, BLOCK_ROWS, BLOCK_COLS), jnp.int32),
            pltpu.SemaphoreType.DMA((2,)),
            pltpu.SemaphoreType.DMA((ARRIVALS,)),
            pltpu.SemaphoreType.DMA((5,)),
        ],
        compiler_params=pltpu.CompilerParams(
            collective_id=0, has_side_effects=True, vmem_limit_bytes=48 * 1024 * 1024
        ),
        name="commutator",
    )(*arrays)


def solution(mesh):
    return jax.shard_map(
        shards,
        mesh=mesh,
        in_specs=(
            P("row", "col"),
            P("row", "col"),
            P("row", "col"),
            P("row", "col"),
            P("row", "col"),
        ),
        out_specs=P("row", "col"),
        check_vma=False,
    )
```

```python
import functools

import jax
import jax.numpy as jnp
from jax import lax
from jax.experimental import pallas as pl
from jax.experimental.pallas import tpu as pltpu
from jax.sharding import PartitionSpec as P

MESH = pl.DeviceIdType.MESH
ROWS = 384
COLS = 768
BLOCK = 64
BLOCK_ROWS = ROWS // BLOCK
BLOCK_COLS = COLS // BLOCK
CUTS = (0, 128, 192, 256, 384)
CHUNKS = tuple(zip(CUTS[:-1], CUTS[1:]))
WHOLE = (0, ROWS)
ROW_EDGE = 64
COL_EDGE = 32
TAIL = 128
ARRIVALS = 43


def device_of(x, y, z, core):
    return (4 * z + 2 * (y // 2) + core, 2 * x + y % 2)


def spread(pattern):
    block_of = lax.broadcasted_iota(jnp.int32, (BLOCK_COLS, COLS), 1) // BLOCK
    index = lax.broadcasted_iota(jnp.int32, (BLOCK_COLS, COLS), 0)
    select = jnp.where(block_of == index, 1.0, 0.0).astype(jnp.float32)
    return jnp.dot(pattern.astype(jnp.float32), select, preferred_element_type=jnp.float32)


class Gather:
    def __init__(self, copy, arrival, part, place, low, ahead, behind, crossed, edge):
        self.copy, self.part, self.place, self.low = copy, part, place, low
        self.ahead, self.behind, self.crossed = ahead, behind, crossed
        self.low_edge = (ROWS - 2 * edge, ROWS - edge)
        self.high_edge = (ROWS - edge, ROWS)
        first, second, third, fourth, last = (arrival() for _ in range(5))
        self.from_behind = {(False, 0): first, (False, 1): second, (False, 2): last, (False, 3): last}
        self.from_ahead = {(False, 3): third, (False, 2): fourth, (False, 1): last, (False, 0): last}
        first, second, middle, last = (arrival() for _ in range(4))
        self.from_behind.update({(True, 3): first, (True, 1): middle, (True, 2): middle, (True, 0): last})
        self.from_ahead.update({(True, 3): second, (True, 1): middle, (True, 2): middle, (True, 0): last})
        outer, inner = arrival(), arrival()
        self.far = {0: outer, 3: outer, 1: inner, 2: inner}
        self.far_crossed, self.far_middle, self.far_edges = (arrival() for _ in range(3))

    def k(self, offset, other):
        low = 1 - self.low if other else self.low
        return 2 * ((self.place + offset) % 4) + low

    def piece(self, offset, other, span):
        return self.part(self.k(offset, other), *span)

    def move(self, offset, other, span, target, arrival):
        piece = self.piece(offset, other, span)
        self.copy(piece, piece, target, span, arrival)

    def send_ahead(self, other, c):
        self.move(0, other, CHUNKS[c], self.ahead, self.from_behind[other, c])

    def send_behind(self, other, c):
        self.move(0, other, CHUNKS[c], self.behind, self.from_ahead[other, c])

    def pass_ahead(self, c):
        self.move(3, False, CHUNKS[c], self.ahead, self.far[c])

    def pass_behind(self, c):
        self.move(1, False, CHUNKS[c], self.behind, self.far[c])

    def pass_edges(self):
        self.from_behind[True, 3].wait()
        self.move(3, True, self.low_edge, self.ahead, self.far_edges)
        self.from_ahead[True, 3].wait()
        self.move(1, True, self.high_edge, self.behind, self.far_edges)

    def cross_far(self, c, target):
        span = (CHUNKS[c][0], min(CHUNKS[c][1], self.low_edge[0]))
        if span[0] == span[1]:
            return
        if c in self.crossed:
            arrival = self.far_crossed
        else:
            arrival = self.far_edges if c == 3 else self.far_middle
        self.move(2, False, span, target, arrival)


def kernel(ham, den, h_pat, p_pat, keep, out, row, col, acc, kept, tiles, pats, send, recv, load):
    row_index = lax.axis_index("row")
    col_index = lax.axis_index("col")
    x, y_lo = col_index // 2, col_index % 2
    z, y_hi, core = row_index // 4, (row_index // 2) % 2, row_index % 2
    y = 2 * y_hi + y_lo
    right = device_of((x + 1) % 4, y, z, core)
    left = device_of((x + 3) % 4, y, z, core)
    up = device_of(x, y, (z + 1) % 4, core)
    down = device_of(x, y, (z + 3) % 4, core)
    beside = device_of(x, 2 * y_hi + 1 - y_lo, z, core)
    across = device_of(x, 2 * (1 - y_hi) + y_lo, z, core)
    opposite = device_of(x, 3 - y, z, core)
    sibling = device_of(x, y, z, 1 - core)

    barrier = pltpu.get_barrier_semaphore()
    partners = (right, left, up, down, beside, across, opposite, sibling)
    for partner in partners:
        pl.semaphore_signal(barrier, inc=1, device_id=partner, device_id_type=MESH)

    loads = []
    pairs = (
        (h_pat, pats.at[0]),
        (ham, tiles.at[0]),
        (p_pat, pats.at[1]),
        (den, tiles.at[1]),
        (keep, pats.at[2]),
    )
    for i, (source, target) in enumerate(pairs):
        made = pltpu.make_async_copy(source, target, load.at[i])
        made.start()
        loads.append(made)

    row_own = 2 * x + y_lo
    col_own = 2 * z + y_hi
    base = core * ROWS
    for matrix in range(2):
        loads[2 * matrix].wait()
        loads[2 * matrix + 1].wait()
        mask = spread(pats[matrix]).astype(jnp.bfloat16)
        for i in range(BLOCK_ROWS):
            rows = pl.ds(i * BLOCK, BLOCK)
            masked = tiles[matrix, rows, :] * mask[i : i + 1, :]
            row[row_own, matrix, rows, :] = masked
            col[col_own, matrix, pl.ds(pl.multiple_of(base + i * BLOCK, BLOCK), BLOCK), :] = masked
    loads[4].wait()
    pl.semaphore_wait(barrier, len(partners))

    def extent(count):
        if count <= 2 * ROWS:
            return col.at[0, :, pl.ds(0, count), :]
        if count <= 8 * ROWS:
            return row.at[pl.ds(0, count // ROWS)]
        return col.at[pl.ds(0, count // (2 * ROWS))]

    def described(source, landing, target, sender, arrival):
        return pltpu.make_async_remote_copy(
            src_ref=source,
            dst_ref=landing,
            send_sem=send.at[sender],
            recv_sem=recv.at[arrival],
            device_id=target,
            device_id_type=MESH,
        )

    arrivals = []

    class Arrival:
        def __init__(self):
            self.index, self.count = len(arrivals), 0
            arrivals.append(self)

        def wait(self):
            if self.count:
                area = extent(self.count)
                described(area, area, sibling, 0, self.index).wait_recv()
                self.count = 0

    sent = [0, 0]

    def copier(sender):
        def copy(source, landing, target, span, arrival):
            arrival.count += span[1] - span[0]
            sent[sender] += span[1] - span[0]
            described(source, landing, target, sender, arrival.index).start()

        return copy

    copy_row, copy_col = copier(0), copier(1)

    def row_part(k, first, last):
        return row.at[k, :, pl.ds(first, last - first), :]

    def col_part(k, first, last):
        start = pl.multiple_of(base + first, 16)
        return col.at[k, :, pl.ds(start, last - first), :]

    rows = Gather(copy_row, Arrival, row_part, x, y_lo, right, left, (0, 1, 2), ROW_EDGE)
    cols = Gather(copy_col, Arrival, col_part, z, y_hi, up, down, (0,), COL_EDGE)
    both = (rows, cols)
    crossed = [Arrival() for _ in CHUNKS]
    turned = [Arrival() for _ in CHUNKS]
    shared = [Arrival() for _ in range(7)]

    def share(stage, offset, other, span):
        cols.move(offset, other, span, sibling, shared[stage])

    def cross(c):
        rows.move(0, False, CHUNKS[c], beside, crossed[c])

    def turn(c):
        crossed[c].wait()
        landing = col_part(col_own, *CHUNKS[c])
        copy_row(rows.piece(0, True, CHUNKS[c]), landing, opposite, CHUNKS[c], turned[c])

    def kind_of(place, low, k):
        distance = (k // 2 - place + 4) % 4
        other = (k % 2 + low) % 2
        late = jnp.where(distance == 2, 2, 1)
        return jnp.where((other == 0) | (distance == 0), 0, late)

    def product(k, out_part, inner_part):
        out_span = slice(*out_part)
        if inner_part == WHOLE:
            inner_spans = [slice(None)]
        else:
            inner_spans = [slice(base + inner_part[0], base + inner_part[1]) for base in (0, ROWS)]

        def left(matrix):
            pieces = [row[k, matrix, out_span, inner] for inner in inner_spans]
            return jnp.concatenate(pieces, axis=1)

        def right(matrix):
            return jnp.concatenate([col[k, matrix, inner, :] for inner in inner_spans], axis=0)

        forward = jnp.dot(left(0), right(1), preferred_element_type=jnp.float32)
        backward = jnp.dot(left(1), right(0), preferred_element_type=jnp.float32)
        acc[out_span, :] += forward - backward

    def visit(k, r, c, entries):
        for row_kinds, col_kinds, *parts in entries:
            fits = [(r == kind) & (c == other) for kind in row_kinds for other in col_kinds]

            @pl.when(functools.reduce(jnp.logical_or, fits))
            def _():
                for out_part, inner_part in parts:
                    product(k, out_part, inner_part)

    def stage(*entries):
        @pl.loop(0, 8)
        def _(k):
            visit(k, kind_of(x, y_lo, k), kind_of(z, y_hi, k), entries)

    def stage_of(g, kind, *entries):
        def body(offset):
            k = g.k(offset, True)
            if g is rows:
                visit(k, kind, kind_of(z, y_hi, k), entries)
            else:
                visit(k, kind_of(x, y_lo, k), kind, entries)

        if kind == 2:
            body(2)
        else:

            @pl.loop(0, 2)
            def _(i):
                body(1 + 2 * i)

    near_first, near_last = (TAIL, ROWS), (0, TAIL)
    far_rows_first, far_rows_last = (0, 2 * TAIL), (2 * TAIL, ROWS)
    far_cols_first, far_cols_last = (0, TAIL), (TAIL, ROWS)

    for first, second in ((0, 3), (1, 2)):
        for g in both:
            g.send_ahead(False, first)
            g.send_behind(False, second)
        if first == 0:
            cross(3)
            cross(1)
    cross(2)
    cross(0)
    share(0, 0, False, WHOLE)
    acc[...] = jnp.zeros_like(acc)
    kept[...] = spread(pats[2])

    for first, second in ((0, 3), (1, 2)):
        for g in both:
            g.from_behind[False, first].wait()
            g.pass_ahead(first)
            g.from_ahead[False, second].wait()
            g.pass_behind(second)
        if first == 0:
            turn(3)
    for first, second in ((2, 1), (3, 0)):
        for g in both:
            g.send_ahead(False, first)
            g.send_behind(False, second)
    turn(1)
    turn(2)

    def cross_far(g, target, *chunks):
        for c in chunks:
            g.far[c].wait()
            g.cross_far(c, target)

    cross_far(rows, beside, 0)
    turn(0)
    for c in (3, 1, 2):
        rows.send_ahead(True, c)
        rows.send_behind(True, c)
    cross_far(rows, beside, 1, 2, 3)
    for c in (3, 1, 2, 0):
        turned[c].wait()
        cols.send_ahead(True, c)
        cols.send_behind(True, c)
    share(0, 0, True, WHOLE)
    cross_far(cols, across, 0, 1, 2, 3)
    share(0, 2, False, WHOLE)
    for g in both:
        g.from_behind[False, 3].wait()
    share(0, 3, False, WHOLE)
    share(0, 1, False, WHOLE)
    rows.pass_edges()
    rows.send_ahead(True, 0)
    rows.send_behind(True, 0)
    cols.pass_edges()
    shared[0].wait()
    stage(((0,), (0,), (WHOLE, WHOLE)))

    rows.far_crossed.wait()
    stage_of(rows, 2, ((2,), (0,), (far_rows_first, WHOLE)))

    cols.from_behind[True, 1].wait()
    share(1, 3, True, near_first)
    share(1, 1, True, near_first)
    cols.far_crossed.wait()
    share(2, 2, True, far_cols_first)
    rows.from_behind[True, 1].wait()
    shared[1].wait()
    shared[2].wait()
    stage(
        ((1,), (0,), (near_first, WHOLE)),
        ((0,), (1,), (WHOLE, near_first)),
        ((1,), (1,), (near_first, near_first)),
        ((2,), (1,), (far_rows_first, near_first)),
        ((0,), (2,), (WHOLE, far_cols_first)),
        ((1,), (2,), (near_first, far_cols_first)),
        ((2,), (2,), (far_rows_first, far_cols_first)),
    )

    rows.far_edges.wait()
    stage_of(
        rows,
        2,
        ((2,), (0,), (far_rows_last, WHOLE)),
        ((2,), (1,), (far_rows_last, near_first)),
        ((2,), (2,), (far_rows_last, far_cols_first)),
    )

    cols.from_behind[True, 0].wait()
    share(3, 1, True, near_last)
    share(5, 3, True, near_last)
    for arrived, offset in ((3, 1), (5, 3)):
        shared[arrived].wait()
        k = cols.k(offset, True)
        visit(
            k,
            kind_of(x, y_lo, k),
            1,
            (
                ((0, 2), (1,), (WHOLE, near_last)),
                ((1,), (1,), (near_first, near_last)),
            ),
        )
        if offset == 1:
            cols.far_middle.wait()
            share(6, 2, True, (TAIL, 2 * TAIL))

    cols.far_edges.wait()
    share(4, 2, True, (2 * TAIL, ROWS))
    rows.from_behind[True, 0].wait()
    stage_of(
        rows,
        1,
        ((1,), (0, 1), (near_last, WHOLE)),
        ((1,), (2,), (near_last, far_cols_first)),
    )
    shared[6].wait()
    shared[4].wait()
    product(cols.k(2, True), WHOLE, far_cols_last)

    for i in range(BLOCK_ROWS):
        block_rows = pl.ds(i * BLOCK, BLOCK)
        out[block_rows, :] = acc[block_rows, :] * kept[i : i + 1, :]
    for sender, count in enumerate(sent):
        area = extent(count)
        described(area, area, sibling, sender, 0).wait_send()


def shards(*arrays):
    arrays = [pltpu.with_memory_space_constraint(array, pltpu.HBM) for array in arrays]
    return pl.pallas_call(
        kernel,
        out_shape=jax.ShapeDtypeStruct((ROWS, COLS), jnp.float32),
        in_specs=[pl.BlockSpec(memory_space=pl.ANY)] * 5,
        out_specs=pl.BlockSpec(memory_space=pltpu.VMEM),
        scratch_shapes=[
            pltpu.VMEM((8, 2, ROWS, COLS), jnp.bfloat16),
            pltpu.VMEM((8, 2, 2 * ROWS, COLS), jnp.bfloat16),
            pltpu.VMEM((ROWS, COLS), jnp.float32),
            pltpu.VMEM((BLOCK_ROWS, COLS), jnp.float32),
            pltpu.VMEM((2, ROWS, COLS), jnp.bfloat16),
            pltpu.VMEM((3, BLOCK_ROWS, BLOCK_COLS), jnp.int32),
            pltpu.SemaphoreType.DMA((2,)),
            pltpu.SemaphoreType.DMA((ARRIVALS,)),
            pltpu.SemaphoreType.DMA((5,)),
        ],
        compiler_params=pltpu.CompilerParams(
            collective_id=0, has_side_effects=True, vmem_limit_bytes=48 * 1024 * 1024
        ),
        name="commutator",
    )(*arrays)


def solution(mesh):
    return jax.shard_map(
        shards,
        mesh=mesh,
        in_specs=(
            P("row", "col"),
            P("row", "col"),
            P("row", "col"),
            P("row", "col"),
            P("row", "col"),
        ),
        out_specs=P("row", "col"),
        check_vma=False,
    )
```
